256 devices in a mesh: leaf: 16 (over x, y), blk: 16 (over z, core).
Axes of the slice: x: 4, y: 4, z: 8, core: 2. Of those that a mesh axis runs over, the one named last changes fastest.
Arguments:
- rhs_root: float32 [128, 16384], P(None, ('leaf', 'blk')), may hold values from -6 to 6
- rhs_one: float32 [128, 16384], P(None, ('leaf', 'blk')), may hold values from -6 to 6
- rhs_two: float32 [128, 16384], P(None, ('leaf', 'blk')), may hold values from -6 to 6
- inv_root: bfloat16 [16384, 16384], P(('leaf', 'blk'))
- inv_one: bfloat16 [16384, 8192], P(('leaf', 'blk'))
- inv_two: bfloat16 [16384, 4096], P(('leaf', 'blk'))
- lower_one: bfloat16 [16384, 8192], P(('leaf', 'blk')), may hold values from -0.03125 to 0.03125
- lower_two: bfloat16 [16384, 8192], P(('leaf', 'blk')), may hold values from -0.046875 to 0.046875
- rows_one: int32 [2, 8192], replicated, may hold values from 0 to 16383, as said below
- rows_two: int32 [4, 8192], replicated, may hold values from 0 to 24575, as said below
- count_one: int32 [2], replicated, may hold values from 1 to 8192, 10240 in all
- count_two: int32 [4], replicated, may hold values from 1 to 8192, 20480 in all
Outputs:
- sol_root: float32 [128, 16384], P(None, ('leaf', 'blk'))
- sol_one: float32 [128, 16384], P(None, ('leaf', 'blk'))
- sol_two: float32 [128, 16384], P(None, ('leaf', 'blk'))
The draws below stay inside these ranges and needn't reach their ends.
Inputs may be any that keep to these rules, and one draw needn't show every extreme that they name: `rows_one`: each list holds 8192 distinct rows of the root, among them the root's first and last row. `rows_two`: each list holds 8192 distinct positions among the root's 16384 rows followed by the parent's 8192 rows, among them the first and the last. `count_one`: the counts sum to 10240. `count_two`: the counts sum to 20480.
All inputs are finite; a program needn't handle non-finite values.
Results may differ from the reference program's by a relative error of at most 0.0041.
Values may be sent and summed in bfloat16 or wider, within the bound.
A program may use at most 128 MiB of HBM per device.

```python
import math
import jax
import jax.numpy as jnp
import numpy as np

VECS = 128
W_ROOT = 16384
W_ONE = 8192
W_TWO = 4096
R_ONE = 8192
R_TWO = 8192


def triangle(noise, diag_values, sep_width):
    row_total = noise.shape[0]
    within = (jnp.arange(row_total) % sep_width)[:, None]
    column = jnp.arange(sep_width)[None, :]
    lower_part = jnp.where(column < within, noise * sep_width ** (-0.5), 0.0)
    return (lower_part + jnp.where(column == within, diag_values[:, None], 0.0)).astype(jnp.bfloat16)


def ancestor_rows(key, sep_count, anc_span, list_len):
    keys = jax.random.split(key, sep_count)

    def single(one_key):
        key_one, key_two = jax.random.split(one_key)
        inner = 1 + jax.random.permutation(key_one, anc_span - 2)[:list_len - 2]
        picked = jnp.concatenate([jnp.array([0, anc_span - 1], jnp.int32), inner.astype(jnp.int32)])
        return picked[jax.random.permutation(key_two, list_len)]
    return jax.vmap(single)(keys)


def draw_inv_root(key, part):
    key = jax.random.fold_in(key, 1)
    key_one, key_two = jax.random.split(key)
    noise = jax.random.normal(key_one, (W_ROOT, W_ROOT), jnp.float32)
    diag_values = jax.random.uniform(key_two, (W_ROOT,), jnp.float32, 0.6, 1.4)
    return triangle(noise, diag_values, W_ROOT)


def draw_inv_one(key, part):
    key = jax.random.fold_in(key, 2)
    key_one, key_two = jax.random.split(key)
    noise = jax.random.normal(key_one, (2 * W_ONE, W_ONE), jnp.float32)
    diag_values = jax.random.uniform(key_two, (2 * W_ONE,), jnp.float32, 0.6, 1.4)
    return triangle(noise, diag_values, W_ONE)


def draw_inv_two(key, part):
    key = jax.random.fold_in(key, 3)
    key_one, key_two = jax.random.split(key)
    noise = jax.random.normal(key_one, (4 * W_TWO, W_TWO), jnp.float32)
    diag_values = jax.random.uniform(key_two, (4 * W_TWO,), jnp.float32, 0.6, 1.4)
    return triangle(noise, diag_values, W_TWO)


def draw_rows_one(key, part):
    key = jax.random.fold_in(key, 11)
    return ancestor_rows(key, 2, W_ROOT, R_ONE)


def draw_rows_two(key, part):
    key = jax.random.fold_in(key, 12)
    return ancestor_rows(key, 4, W_ROOT + W_ONE, R_TWO)


def shard_levels(key, shape, cuts, smallest, top_value):
    loudness = 1.0
    for axis_at, blocks in cuts:
        heights = jax.random.uniform(jax.random.fold_in(jax.random.fold_in(key, 6), axis_at), (blocks,), jnp.float32, smallest / len(cuts), top_value / len(cuts))
        loudness = loudness * jnp.repeat(jnp.exp(heights), shape[axis_at] // blocks).reshape((-1,) + (1,) * (len(shape) - 1 - axis_at))
    return loudness


def profile(count, total, reach, lean):
    portions = [(1 << 20) // math.isqrt(rank ** lean) + 1 for rank in range(2, count + 1)]
    rest, holding = total - reach - (count - 1), [1] * (count - 1)
    while rest > 0:
        movable = [i for i in range(count - 1) if holding[i] < reach]
        whole, remaining = sum([portions[i] for i in movable]), rest
        for i in movable:
            addition = min(reach - holding[i], max(1, remaining * portions[i] // whole), rest)
            holding[i] = holding[i] + addition
            rest = rest - addition
    return np.array([reach] + holding)


def ragged_sizes(own_key, amount, total, bound, lean):
    if amount == 2:
        one = jax.random.randint(own_key, (), max(1, total - bound), min(bound, total - 1) + 1)
        return jnp.stack([one, total - one])
    sizes = jnp.asarray(profile(amount, total, bound, lean), jnp.int32)
    pairs = (amount - 1) // 2
    giver, taker = sizes[1:1 + 2 * pairs:2], sizes[2:2 + 2 * pairs:2]
    margin = jnp.minimum(giver - 1, bound - taker)
    moved = jax.random.randint(jax.random.fold_in(own_key, 1), (pairs,), 0, 1 << 20) % (margin + 1)
    sizes = sizes.at[1:1 + 2 * pairs:2].set(giver - moved).at[2:2 + 2 * pairs:2].set(taker + moved)
    return sizes[jax.random.permutation(jax.random.fold_in(own_key, 2), amount)]


def normal_values(key, extent, width, most, cuts=(), kind=jnp.bfloat16):
    drawn = width * jax.random.normal(key, extent, jnp.float32)
    if cuts:
        drawn = drawn * shard_levels(key, extent, cuts, -0.22, 0.18)
    return jnp.clip(drawn, -most, most).astype(kind)


def setup_inputs(seed: int = 0) -> dict:
    arg_keys = jax.random.split(jax.random.key(seed), 13)
    return {
        "rhs_root": normal_values(arg_keys[0], (VECS, W_ROOT), 1.0, 6.0, ((1, 256),), jnp.float32),
        "rhs_one": normal_values(arg_keys[1], (VECS, 2 * W_ONE), 1.0, 6.0, ((1, 256),), jnp.float32),
        "rhs_two": normal_values(arg_keys[2], (VECS, 4 * W_TWO), 1.0, 6.0, ((1, 256),), jnp.float32),
        "inv_root": draw_inv_root(jax.random.fold_in(arg_keys[12], 71), 0),
        "inv_one": draw_inv_one(jax.random.fold_in(arg_keys[12], 71), 0),
        "inv_two": draw_inv_two(jax.random.fold_in(arg_keys[12], 71), 0),
        "lower_one": normal_values(arg_keys[6], (2 * W_ONE, R_ONE), (4 * W_ONE) ** -0.5, 0.03125, ((0, 256),)),
        "lower_two": normal_values(arg_keys[7], (4 * W_TWO, R_TWO), (4 * W_TWO) ** -0.5, 0.046875, ((0, 256),)),
        "rows_one": draw_rows_one(jax.random.fold_in(arg_keys[12], 71), 0),
        "rows_two": draw_rows_two(jax.random.fold_in(arg_keys[12], 71), 0),
        "count_one": ragged_sizes(arg_keys[10], 2, 5 * 2 * R_ONE // 8, R_ONE, 2).astype(jnp.int32),
        "count_two": ragged_sizes(arg_keys[11], 4, 5 * 4 * R_TWO // 8, R_TWO, 2).astype(jnp.int32),
    }


def level_solve(rhs_bf, inverse, sep_width):
    sep_count = rhs_bf.shape[1] // sep_width
    pieces = []
    for member in range(sep_count):
        rhs_block = rhs_bf[:, member * sep_width:(member + 1) * sep_width]
        inv_block = inverse[member * sep_width:(member + 1) * sep_width]
        pieces.append(jnp.dot(rhs_block, inv_block.T, preferred_element_type=jnp.float32))
    return jnp.concatenate(pieces, axis=1)


def spread(y_bf, lower, row_lists, row_counts, sep_width, anc_span):
    sep_count = y_bf.shape[1] // sep_width
    moved = []
    for member in range(sep_count):
        update_terms = jnp.dot(y_bf[:, member * sep_width:(member + 1) * sep_width],
                               lower[member * sep_width:(member + 1) * sep_width],
                               preferred_element_type=jnp.float32)
        live_mask = jnp.arange(update_terms.shape[1], dtype=jnp.int32) < row_counts[member]
        update_terms = jnp.where(live_mask[None, :], update_terms, jnp.zeros_like(update_terms))
        dense = jnp.zeros((update_terms.shape[0], anc_span), jnp.float32)
        moved.append(dense.at[:, row_lists[member]].add(-update_terms))
    return moved


def reference(rhs_root, rhs_one, rhs_two, inv_root, inv_one, inv_two, lower_one, lower_two, rows_one, rows_two, count_one, count_two):
    sol_two = level_solve(rhs_two.astype(jnp.bfloat16), inv_two, W_TWO)
    moved_two = spread(sol_two.astype(jnp.bfloat16), lower_two, rows_two, count_two, W_TWO, W_ROOT + W_ONE)
    acc_root = rhs_root
    acc_one = rhs_one
    for member in range(4):
        acc_root = acc_root + moved_two[member][:, :W_ROOT]
        parent = member // 2
        acc_one = acc_one.at[:, parent * W_ONE:(parent + 1) * W_ONE].add(moved_two[member][:, W_ROOT:])
    sol_one = level_solve(acc_one.astype(jnp.bfloat16), inv_one, W_ONE)
    moved_one = spread(sol_one.astype(jnp.bfloat16), lower_one, rows_one, count_one, W_ONE, W_ROOT)
    for member in range(2):
        acc_root = acc_root + moved_one[member]
    sol_root = level_solve(acc_root.astype(jnp.bfloat16), inv_root, W_ROOT)
    return (sol_root, sol_one, sol_two)
```

```python
import functools

import jax
import jax.numpy as jnp
from jax import lax
from jax.experimental import pallas as pl
from jax.experimental.pallas import tpu as pltpu
from jax.sharding import PartitionSpec as P

VECS = 128
WIDTH = 64
MESH = pl.DeviceIdType.MESH
NX, NY, NZ, NC = 4, 4, 8, 2
ROOT_SLABS = NX * NY
UNROLL = 32


def place_kernel(rows_two, rows_one, live, lower_two, lower_one, out, source, placed):
    length = lower_two.shape[1]
    step = 512

    def turn(i, carry):
        cols = pl.ds(pl.multiple_of(i * step, step), step)
        both = jnp.concatenate([lower_two[:, cols], lower_one[:, cols]], axis=0)
        source[cols, :] = both.astype(jnp.float32).T
        return carry

    lax.fori_loop(0, length // step, turn, 0)

    def clear(i, carry):
        placed[pl.ds(pl.multiple_of(i * step, step), step), :] = jnp.zeros((step, 2 * WIDTH), jnp.float32)
        return carry

    lax.fori_loop(0, placed.shape[0] // step, clear, 0)

    def move(rows, count, lanes):
        def many(i, carry):
            base = pl.multiple_of(i * UNROLL, UNROLL)
            targets = [rows[base + k] for k in range(UNROLL)]
            values = [source[pl.ds(base + k, 1), lanes] for k in range(UNROLL)]
            for k in range(UNROLL):
                placed[pl.ds(targets[k], 1), lanes] = values[k]
            return carry

        def one(j, carry):
            placed[pl.ds(rows[j], 1), lanes] = source[pl.ds(j, 1), lanes]
            return carry

        whole = count // UNROLL
        lax.fori_loop(0, whole, many, 0)
        lax.fori_loop(whole * UNROLL, count, one, 0)

    move(rows_two, live[0], slice(0, WIDTH))
    move(rows_one, live[1], slice(WIDTH, 2 * WIDTH))

    def narrow(i, carry):
        part = placed[pl.ds(pl.multiple_of(i * step, step), step), :].astype(jnp.bfloat16)
        out[pl.ds(i * (step // 128), step // 128)] = part.reshape(step // 128, NC, WIDTH, 2 * WIDTH)
        return carry

    lax.fori_loop(0, placed.shape[0] // step, narrow, 0)


def place(rows_two, rows_one, live, lower_two, lower_one, span):
    smem = pl.BlockSpec(memory_space=pltpu.SMEM)
    vmem = pl.BlockSpec(memory_space=pltpu.VMEM)
    return pl.pallas_call(
        place_kernel,
        out_shape=jax.ShapeDtypeStruct((span // 128, NC, WIDTH, 2 * WIDTH), jnp.bfloat16),
        in_specs=[smem, smem, smem, vmem, vmem],
        out_specs=vmem,
        scratch_shapes=[
            pltpu.VMEM((lower_two.shape[1], 2 * WIDTH), jnp.float32),
            pltpu.VMEM((span, 2 * WIDTH), jnp.float32),
        ],
        compiler_params=pltpu.CompilerParams(vmem_limit_bytes=48 * 2**20),
    )(rows_two, rows_one, live, lower_two, lower_one)


def turned_in(piece):
    padded = jnp.concatenate([piece, jnp.zeros_like(piece)], axis=1)
    return padded.T[:WIDTH]


def turned_out(piece):
    padded = jnp.concatenate([piece, jnp.zeros_like(piece)], axis=0)
    return padded.T[:, :WIDTH]


def main_kernel(
    rhs_root, rhs_one, rhs_two, inv_root_hbm, inv_one_hbm, inv_two_hbm, placed_hbm,
    sol_root, sol_one, sol_two,
    inv_root, inv_one, inv_two, placed,
    full_two, full_one, full_root,
    give_one, take_one, sum_one, ra_one, tb_one, rb_one, vz_one, rz_one,
    give_root, take_root, sum_root, ra_root, tb_root, rb_root, vz_root, rz_root,
    local_sems, z_sems, a_sems, b_sems, s_sems, rs_z_sems, rs_a_sems, rs_b_sems, rs_s_sems,
):
    leaf = lax.axis_index("leaf")
    blk = lax.axis_index("blk")
    x, y = leaf // NY, leaf % NY
    z, c = blk // NC, blk % NC
    half, pair = x // 2, x % 2
    other = 1 - c

    def z_peer(at):
        return (leaf, at * NC + c)

    sibling = (leaf, z * NC + other)

    loads = [
        pltpu.make_async_copy(inv_two_hbm, inv_two, local_sems.at[0]),
        pltpu.make_async_copy(placed_hbm, placed, local_sems.at[1]),
        pltpu.make_async_copy(inv_one_hbm, inv_one, local_sems.at[2]),
        pltpu.make_async_copy(inv_root_hbm, inv_root, local_sems.at[3]),
    ]
    for load in loads:
        load.start()

    barrier = pltpu.get_barrier_semaphore()
    greeted = [z_peer((z + o) % NZ) for o in range(1, NZ)]
    greeted += [(x * NY + (y + o) % NY, blk) for o in range(1, NY)]
    greeted += [((x + o) % NX * NY + y, blk) for o in range(1, NX)]
    greeted += [sibling]
    for device in greeted:
        pl.semaphore_signal(barrier, inc=1, device_id=device, device_id_type=MESH)

    def remote(source, target, sems, index, device):
        return pltpu.make_async_remote_copy(
            src_ref=source,
            dst_ref=target,
            send_sem=sems.at[(0, *index)],
            recv_sem=sems.at[(1, *index)],
            device_id=device,
            device_id_type=MESH,
        )

    def axes_of(core, nx):
        mine_x = pair if nx == 2 else (x if nx == 4 else 0)

        def x_peer(o):
            to = half * 2 + (pair + o) % 2 if nx == 2 else (x + o) % NX
            return (to * NY + y, blk)

        def y_peer(o):
            return (x * NY + (y + o) % NY, blk)

        along_x = (nx, mine_x, x_peer)
        along_y = (NY, y, y_peer)
        if core == 0:
            return along_y, along_x, lambda a, b: b * NY + a
        return along_x, along_y, lambda a, b: a * NY + b

    def by_core(body):
        for core in range(NC):
            pl.when(c == core)(functools.partial(body, core))

    def gather(level, nx, full):
        mine_x = pair if nx == 2 else (x if nx == 4 else 0)
        own = mine_x * NY + y

        def z_copy(o):
            return remote(full.at[own, z, c], full.at[own, z, c], z_sems, (level, o), z_peer((z + o) % NZ))

        def z_arrival(o):
            at = (z + NZ - o) % NZ
            return remote(full.at[own, at, c], full.at[own, at, c], z_sems, (level, o), z_peer(at))

        for o in range(1, NZ):
            z_copy(o).start()
        for o in range(1, NZ):
            z_arrival(o).wait_recv()

        def forward(slab):
            return remote(full.at[slab, :, c], full.at[slab, :, c], s_sems, (level, slab), sibling)

        def planes(core, finish):
            (na, a, a_peer), (nb, b, b_peer), slab_of = axes_of(core, nx)

            def slab_at(oa, ob):
                return slab_of((a + na - oa) % na, (b + nb - ob) % nb)

            def a_copy(oa, slab):
                return remote(full.at[slab, :, c], full.at[slab, :, c], a_sems, (level, oa), a_peer(oa))

            def b_copy(oa, ob, slab):
                return remote(full.at[slab, :, c], full.at[slab, :, c], b_sems, (level, oa, ob), b_peer(ob))

            if finish:
                for oa in range(1, na):
                    a_copy(oa, own).wait_send()
                for oa in range(na):
                    for ob in range(1, nb):
                        b_copy(oa, ob, slab_at(oa, 0)).wait_send()
                return
            for oa in range(1, na):
                a_copy(oa, own).start()
            for ob in range(1, nb):
                b_copy(0, ob, own).start()
            forward(own).start()
            for oa in range(1, na):
                slab = slab_at(oa, 0)
                a_copy(oa, slab).wait_recv()
                for ob in range(1, nb):
                    b_copy(oa, ob, slab).start()
                forward(slab).start()
            for oa in range(na):
                for ob in range(1, nb):
                    slab = slab_at(oa, ob)
                    b_copy(oa, ob, slab).wait_recv()
                    forward(slab).start()

        by_core(lambda core: planes(core, False))

        def finish():
            for o in range(1, NZ):
                z_copy(o).wait_send()
            by_core(lambda core: planes(core, True))
            for slab in range(nx * NY):
                forward(slab).wait_send()

        def arrived(slab):
            remote(full.at[slab, :, other], full.at[slab, :, other], s_sems, (level, slab), sibling).wait_recv()

        return arrived, finish

    def solve(nx, full, inverse, arrived):
        total = jnp.zeros((WIDTH, VECS), jnp.float32)
        wide = NZ * NC * WIDTH
        for slab in range(nx * NY):
            arrived(slab)
            total += jnp.dot(
                inverse[:, slab * wide:(slab + 1) * wide],
                full[slab].reshape(wide, VECS),
                preferred_element_type=jnp.float32,
            )
        return total

    def reduce(level, nx, first, solved, give, take, sums, ra, tb, rb, vz, rz):
        def terms(slab, parity):
            lower = placed[pl.ds((first + slab) * NZ, NZ), parity]
            return jnp.dot(
                lower.reshape(NZ * WIDTH, 2 * WIDTH), solved, preferred_element_type=jnp.float32
            ).reshape(NZ, WIDTH, VECS)

        def pass_on(slab):
            return remote(give.at[slab], take.at[slab], rs_s_sems, (level, slab), sibling)

        def planes(core, finish):
            (na, a, a_peer), (nb, b, b_peer), slab_of = axes_of(core, nx)
            (ma, a2, _), (mb, b2, _), slab_of2 = axes_of(1 - core, nx)

            def a_copy(oa, ob):
                slab = slab_of((a + oa) % na, (b + ob) % nb)
                return remote(sums.at[slab], ra.at[oa - 1, ob], rs_a_sems, (level, oa, ob), a_peer(oa))

            def b_copy(ob):
                return remote(tb.at[ob], rb.at[ob - 1], rs_b_sems, (level, ob), b_peer(ob))

            if finish:
                for ob in range(nb):
                    for oa in range(1, na):
                        a_copy(oa, ob).wait_send()
                for ob in range(1, nb):
                    b_copy(ob).wait_send()
                return
            for ob in [*range(1, mb), 0]:
                for oa in [*range(1, ma), 0]:
                    slab = slab_of2((a2 + oa) % ma, (b2 + ob) % mb)
                    give[slab] = terms(slab, other).astype(jnp.bfloat16)
                    pass_on(slab).start()
            for ob in [*range(1, nb), 0]:
                for oa in [*range(1, na), 0]:
                    slab = slab_of((a + oa) % na, (b + ob) % nb)
                    part = terms(slab, c)
                    pass_on(slab).wait_recv()
                    sums[slab] = (part + take[slab].astype(jnp.float32)).astype(jnp.bfloat16)
                    if oa:
                        a_copy(oa, ob).start()
            for ob in [*range(1, nb), 0]:
                total = sums[slab_of(a, (b + ob) % nb)].astype(jnp.float32)
                for oa in range(1, na):
                    a_copy(oa, ob).wait_recv()
                    total += ra[oa - 1, ob].astype(jnp.float32)
                if ob:
                    tb[ob] = total.astype(jnp.bfloat16)
                    b_copy(ob).start()
                else:
                    for ob2 in range(1, nb):
                        b_copy(ob2).wait_recv()
                        total += rb[ob2 - 1].astype(jnp.float32)
                    vz[...] = total.astype(jnp.bfloat16)

        by_core(lambda core: planes(core, False))

        def z_copy(o):
            return remote(vz.at[(z + o) % NZ], rz.at[o - 1], rs_z_sems, (level, o), z_peer((z + o) % NZ))

        for o in range(1, NZ):
            z_copy(o).start()
        total = vz[z].astype(jnp.float32)
        for o in range(1, NZ):
            z_copy(o).wait_recv()
            total += rz[o - 1].astype(jnp.float32)

        def finish():
            for o in range(1, NZ):
                z_copy(o).wait_send()
            by_core(lambda core: planes(core, True))
            for slab in range(nx * NY):
                pass_on(slab).wait_send()

        return total, finish

    finishes = []

    full_two[y, z, c] = turned_in(rhs_two[...]).astype(jnp.bfloat16)
    pl.semaphore_wait(barrier, len(greeted))
    arrived, finish = gather(0, 1, full_two)
    finishes.append(finish)
    loads[0].wait()
    solved_two = solve(1, full_two, inv_two, arrived)
    sol_two[...] = turned_out(solved_two)
    y_two = solved_two.astype(jnp.bfloat16)

    loads[1].wait()
    stacked = jnp.concatenate([y_two, jnp.zeros_like(y_two)], axis=0)
    moved, finish = reduce(
        0, 2, ROOT_SLABS, stacked, give_one, take_one, sum_one, ra_one, tb_one, rb_one, vz_one, rz_one
    )
    finishes.append(finish)
    full_one[pair * NY + y, z, c] = (turned_in(rhs_one[...]) - moved).astype(jnp.bfloat16)
    arrived, finish = gather(1, 2, full_one)
    finishes.append(finish)
    loads[2].wait()
    solved_one = solve(2, full_one, inv_one, arrived)
    sol_one[...] = turned_out(solved_one)
    y_one = solved_one.astype(jnp.bfloat16)

    stacked = jnp.concatenate([y_two, y_one], axis=0)
    moved, finish = reduce(
        1, 4, 0, stacked, give_root, take_root, sum_root, ra_root, tb_root, rb_root, vz_root, rz_root
    )
    finishes.append(finish)
    full_root[x * NY + y, z, c] = (turned_in(rhs_root[...]) - moved).astype(jnp.bfloat16)
    arrived, finish = gather(2, 4, full_root)
    finishes.append(finish)
    loads[3].wait()
    sol_root[...] = turned_out(solve(4, full_root, inv_root, arrived))

    for finish in finishes:
        finish()


def substitute(rhs_root, rhs_one, rhs_two, inv_root, inv_one, inv_two, placed):
    vmem = pl.BlockSpec(memory_space=pltpu.VMEM)
    hbm = pl.BlockSpec(memory_space=pl.ANY)
    bf16 = jnp.bfloat16

    def slabs(*lead):
        return pltpu.VMEM((*lead, NZ, WIDTH, VECS), bf16)

    def level(nx):
        return [
            slabs(nx * NY), slabs(nx * NY), slabs(nx * NY),
            slabs(3, NY), slabs(NY), slabs(3),
            slabs(), pltpu.VMEM((NZ - 1, WIDTH, VECS), bf16),
        ]

    sems = pltpu.SemaphoreType.DMA
    out = jax.ShapeDtypeStruct((VECS, WIDTH), jnp.float32)
    return pl.pallas_call(
        main_kernel,
        out_shape=(out, out, out),
        in_specs=[vmem] * 3 + [hbm] * 4,
        out_specs=(vmem,) * 3,
        scratch_shapes=[
            pltpu.VMEM(inv_root.shape, bf16),
            pltpu.VMEM(inv_one.shape, bf16),
            pltpu.VMEM(inv_two.shape, bf16),
            pltpu.VMEM(placed.shape, bf16),
            pltpu.VMEM((NY, NZ, NC, WIDTH, VECS), bf16),
            pltpu.VMEM((2 * NY, NZ, NC, WIDTH, VECS), bf16),
            pltpu.VMEM((NX * NY, NZ, NC, WIDTH, VECS), bf16),
            *level(2),
            *level(4),
            sems((4,)),
            sems((2, 3, NZ)),
            sems((2, 3, 4)),
            sems((2, 3, 4, 4)),
            sems((2, 3, NX * NY)),
            sems((2, 2, NZ)),
            sems((2, 2, 4, 4)),
            sems((2, 2, 4)),
            sems((2, 2, NX * NY)),
        ],
        compiler_params=pltpu.CompilerParams(
            collective_id=0, has_side_effects=True, vmem_limit_bytes=56 * 2**20
        ),
    )(rhs_root, rhs_one, rhs_two, inv_root, inv_one, inv_two, placed)


def shards(
    rhs_root,
    rhs_one,
    rhs_two,
    inv_root,
    inv_one,
    inv_two,
    lower_one,
    lower_two,
    rows_one,
    rows_two,
    count_one,
    count_two,
):
    leaf = lax.axis_index("leaf")
    sep_two = leaf // NY
    sep_one = leaf // (2 * NY)

    def own(array, sep):
        return lax.dynamic_index_in_dim(array, sep, 0, keepdims=False)

    live = jnp.stack([own(count_two, sep_two), own(count_one, sep_one)])
    placed = place(
        own(rows_two, sep_two), own(rows_one, sep_one), live, lower_two, lower_one,
        inv_root.shape[1] + inv_one.shape[1],
    )
    return substitute(rhs_root, rhs_one, rhs_two, inv_root, inv_one, inv_two, placed)


def solution(mesh):
    cut = P(None, ("leaf", "blk"))
    rows = P(("leaf", "blk"), None)
    return jax.shard_map(
        shards,
        mesh=mesh,
        in_specs=(cut, cut, cut, rows, rows, rows, rows, rows, P(), P(), P(), P()),
        out_specs=(cut, cut, cut),
        check_vma=False,
    )
```

```python
import functools

import jax
import jax.numpy as jnp
from jax import lax
from jax.experimental import pallas as pl
from jax.experimental.pallas import tpu as pltpu
from jax.sharding import PartitionSpec as P

VECS = 128
WIDTH = 64
MESH = pl.DeviceIdType.MESH
NX, NY, NZ, NC = 4, 4, 8, 2
ROOT_SLABS = NX * NY
UNROLL = 32
PARTS = 2


def place_kernel(
    rows_two_hbm, rows_one_hbm, count_two, count_one, lower_two_hbm, lower_one_hbm, out_hbm,
    rows_two, rows_one, lower_two, lower_one, source, placed, out, in_sems, out_sems,
):
    leaf = lax.axis_index("leaf")
    sep_two, sep_one = leaf // NY, leaf // (2 * NY)
    loads = [
        pltpu.make_async_copy(lower_two_hbm, lower_two, in_sems.at[0]),
        pltpu.make_async_copy(lower_one_hbm, lower_one, in_sems.at[1]),
        pltpu.make_async_copy(rows_two_hbm.at[sep_two], rows_two, in_sems.at[2]),
        pltpu.make_async_copy(rows_one_hbm.at[sep_one], rows_one, in_sems.at[3]),
    ]
    for load in loads:
        load.start()
    length = lower_two.shape[1]
    step = 512

    def clear(i, carry):
        placed[pl.ds(pl.multiple_of(i * step, step), step), :] = jnp.zeros((step, 2 * WIDTH), jnp.float32)
        return carry

    lax.fori_loop(0, placed.shape[0] // step, clear, 0)
    for load in loads:
        load.wait()

    def turn(i, carry):
        cols = pl.ds(pl.multiple_of(i * step, step), step)
        both = jnp.concatenate([lower_two[:, cols], lower_one[:, cols]], axis=0)
        source[cols, :] = both.astype(jnp.float32).T
        return carry

    lax.fori_loop(0, length // step, turn, 0)

    def move(rows, count, lanes):
        def many(i, carry):
            base = pl.multiple_of(i * UNROLL, UNROLL)
            targets = [rows[base + k] for k in range(UNROLL)]
            values = [source[pl.ds(base + k, 1), lanes] for k in range(UNROLL)]
            for k in range(UNROLL):
                placed[pl.ds(targets[k], 1), lanes] = values[k]
            return carry

        def one(j, carry):
            placed[pl.ds(rows[j], 1), lanes] = source[pl.ds(j, 1), lanes]
            return carry

        whole = count // UNROLL
        lax.fori_loop(0, whole, many, 0)
        lax.fori_loop(whole * UNROLL, count, one, 0)

    move(rows_two, count_two[sep_two], slice(0, WIDTH))
    move(rows_one, count_one[sep_one], slice(WIDTH, 2 * WIDTH))

    chunks = out_sems.shape[0]
    tall = placed.shape[0] // chunks
    stores = []
    for chunk in range(chunks):
        def narrow(i, carry):
            part = placed[pl.ds(pl.multiple_of(i * step, step), step), :].astype(jnp.bfloat16)
            out[pl.ds(i * (step // 128), step // 128)] = part.reshape(step // 128, NC, WIDTH, 2 * WIDTH)
            return carry

        lax.fori_loop(chunk * tall // step, (chunk + 1) * tall // step, narrow, 0)
        piece = slice(chunk * tall // 128, (chunk + 1) * tall // 128)
        stores.append(pltpu.make_async_copy(out.at[piece], out_hbm.at[piece], out_sems.at[chunk]))
        stores[-1].start()
    for store in stores:
        store.wait()


def place(rows_two, rows_one, count_two, count_one, lower_two, lower_one, span):
    smem = pl.BlockSpec(memory_space=pltpu.SMEM)
    hbm = pl.BlockSpec(memory_space=pl.ANY)
    length = lower_two.shape[1]
    result = (span // 128, NC, WIDTH, 2 * WIDTH)
    return pl.pallas_call(
        place_kernel,
        out_shape=jax.ShapeDtypeStruct(result, jnp.bfloat16),
        in_specs=[hbm, hbm, smem, smem, hbm, hbm],
        out_specs=hbm,
        scratch_shapes=[
            pltpu.SMEM((length,), jnp.int32),
            pltpu.SMEM((length,), jnp.int32),
            pltpu.VMEM(lower_two.shape, jnp.bfloat16),
            pltpu.VMEM(lower_one.shape, jnp.bfloat16),
            pltpu.VMEM((length, 2 * WIDTH), jnp.float32),
            pltpu.VMEM((span, 2 * WIDTH), jnp.float32),
            pltpu.VMEM(result, jnp.bfloat16),
            pltpu.SemaphoreType.DMA((4,)),
            pltpu.SemaphoreType.DMA((4,)),
        ],
        compiler_params=pltpu.CompilerParams(vmem_limit_bytes=60 * 2**20),
    )(rows_two, rows_one, count_two, count_one, lower_two, lower_one)


def ring_order(size):
    return {1: (0,), 2: (1, 0), 4: (2, 1, 3, 0)}[size]


def main_kernel(
    rhs_root, rhs_one, rhs_two, inv_root_hbm, inv_one_hbm, inv_two_hbm, placed_hbm,
    sol_root, sol_one, sol_two,
    inv_root, inv_one, inv_two, placed,
    full_two, full_one, full_root,
    *rest,
):
    level_refs = {"one": rest[:11], "root": rest[11:22]}
    local_sems, z_sems, a_sems, b_sems, s_sems, rz_sems, ra_sems, rb_sems, rs_sems = rest[22:]
    leaf = lax.axis_index("leaf")
    blk = lax.axis_index("blk")
    x, y = leaf // NY, leaf % NY
    z, c = blk // NC, blk % NC
    half, pair = x // 2, x % 2
    other = 1 - c
    low, high = slice(0, NZ // 2), slice(NZ // 2, NZ)

    def z_peer(at):
        return (leaf, at * NC + c)

    sibling = (leaf, z * NC + other)

    loads = [
        pltpu.make_async_copy(inv_two_hbm, inv_two, local_sems.at[0]),
        pltpu.make_async_copy(placed_hbm, placed, local_sems.at[1]),
        pltpu.make_async_copy(inv_one_hbm, inv_one, local_sems.at[2]),
        pltpu.make_async_copy(inv_root_hbm, inv_root, local_sems.at[3]),
    ]
    for load in loads:
        load.start()

    barrier = pltpu.get_barrier_semaphore()
    greeted = [z_peer((z + o) % NZ) for o in range(1, NZ)]
    greeted += [(x * NY + (y + o) % NY, blk) for o in (1, 3)]
    greeted += [((x + o) % NX * NY + y, blk) for o in (1, 3)]
    greeted += [sibling]
    for device in greeted:
        pl.semaphore_signal(barrier, inc=1, device_id=device, device_id_type=MESH)

    def remote(source, target, sems, index, device):
        return pltpu.make_async_remote_copy(
            src_ref=source,
            dst_ref=target,
            send_sem=sems.at[(0, *index)],
            recv_sem=sems.at[(1, *index)],
            device_id=device,
            device_id_type=MESH,
        )

    def part_of(h):
        return slice(h * WIDTH // PARTS, (h + 1) * WIDTH // PARTS)

    def axes_of(core, nx):
        mine_x = {1: 0, 2: pair, 4: x}[nx]

        def x_peer(o):
            to = half * 2 + (pair + o) % 2 if nx == 2 else (x + o) % NX
            return (to * NY + y, blk)

        def y_peer(o):
            return (x * NY + (y + o) % NY, blk)

        along_x = (nx, mine_x, x_peer)
        along_y = (NY, y, y_peer)
        first, second = (along_y, along_x) if core == 0 else (along_x, along_y)

        def slab(oa, ob):
            at_a, at_b = (first[1] + oa) % first[0], (second[1] + ob) % second[0]
            return at_b * NY + at_a if core == 0 else at_a * NY + at_b

        return first, second, slab

    def by_core(body):
        for core in range(NC):
            pl.when(c == core)(functools.partial(body, core))

    def gather_steps(core, level, nx, full, sent):
        (na, _, a_peer), (nb, _, b_peer), slab_at = axes_of(core, nx)

        def start(make):
            make().start()
            sent.append(make)

        def steps(h):
            rows = part_of(h)
            own = slab_at(0, 0)

            def piece(at):
                return full.at[own, at, c, rows]

            def z_copy(o):
                return remote(piece(z), piece(z), z_sems, (level, h, o), z_peer((z + o) % NZ))

            def z_arrival(o):
                at = (z + NZ - o) % NZ
                return remote(piece(at), piece(at), z_sems, (level, h, o), z_peer(at))

            def plane(slab, zs, parity=c):
                return full.at[slab, zs, parity, rows]

            def forward(slab):
                start(lambda: remote(plane(slab, slice(None)), plane(slab, slice(None)), s_sems, (level, h, slab), sibling))

            def a_copy(kind, slab):
                zs = (slice(None), slice(None), low, high)[kind]
                return remote(plane(slab, zs), plane(slab, zs), a_sems, (level, h, kind), a_peer((1, -1, 1, -1)[kind] % na))

            def b_copy(oa, kind, slab):
                zs = (slice(None), slice(None), low, high)[kind]
                return remote(
                    plane(slab, zs), plane(slab, zs), b_sems, (level, h, oa, kind), b_peer((1, -1, 1, -1)[kind] % nb)
                )

            def a_send(kind, slab):
                start(lambda: a_copy(kind, slab))

            def b_send(oa, kind, slab):
                start(lambda: b_copy(oa, kind, slab))

            def b_first(oa):
                if nb > 1:
                    b_send(oa, 0, slab_at(oa, 0))
                if nb > 2:
                    b_send(oa, 1, slab_at(oa, 0))

            def step_z():
                for o in range(1, NZ):
                    start(functools.partial(z_copy, o))

            def step_own():
                for o in range(1, NZ):
                    z_arrival(o).wait_recv()
                if na > 1:
                    a_send(0, own)
                if na > 2:
                    a_send(1, own)
                b_first(0)
                forward(own)

            def step_a_near():
                for kind, oa in ((0, na - 1), (1, 1))[: {1: 0, 2: 1, 4: 2}[na]]:
                    slab = slab_at(oa, 0)
                    a_copy(kind, slab).wait_recv()
                    if na > 2:
                        a_send(kind + 2, slab)
                    b_first(oa)
                    forward(slab)

            def step_a_far():
                if na > 2:
                    slab = slab_at(2, 0)
                    a_copy(2, slab).wait_recv()
                    a_copy(3, slab).wait_recv()
                    b_first(2)
                    forward(slab)

            a_order = {1: (0,), 2: (0, 1), 4: (0, 3, 1, 2)}[na]

            def step_b_near():
                for oa in a_order:
                    for kind, ob in ((0, nb - 1), (1, 1))[: {1: 0, 2: 1, 4: 2}[nb]]:
                        slab = slab_at(oa, ob)
                        b_copy(oa, kind, slab).wait_recv()
                        if nb > 2:
                            b_send(oa, kind + 2, slab)
                        forward(slab)

            def step_b_far():
                if nb > 2:
                    for oa in a_order:
                        slab = slab_at(oa, 2)
                        b_copy(oa, 2, slab).wait_recv()
                        b_copy(oa, 3, slab).wait_recv()
                        forward(slab)

            return [step_z, step_own, step_a_near, step_a_far, step_b_near, step_b_far]

        return steps

    def solve(core, level, nx, full, inverse, out):
        (na, _, _), (nb, _, _), slab_at = axes_of(core, nx)
        wide = NZ * NC * WIDTH
        total = jnp.zeros((WIDTH, VECS), jnp.float32)
        for ob in range(nb):
            for oa in range(na):
                slab = slab_at(oa, ob)
                for h in range(PARTS):
                    block = full.at[slab, :, other, part_of(h)]
                    remote(block, block, s_sems, (level, h, slab), sibling).wait_recv()
                total += jnp.dot(
                    inverse[:, pl.ds(pl.multiple_of(slab * wide, wide), wide)],
                    full[slab].reshape(wide, VECS),
                    preferred_element_type=jnp.float32,
                )
        out[...] = total

    def reduce_steps(core, level, nx, first, solved, refs, sent):
        give, take, sums, low_a, high_a, near_a, totals, half_b, near_b, whole, landed = refs
        (na, _, a_peer), (nb, _, b_peer), slab_at = axes_of(core, nx)
        (ma, _, _), (mb, _, _), slab_there = axes_of(1 - core, nx)

        def start(make):
            make().start()
            sent.append(make)

        def terms(slab, parity, rows):
            lower = placed[pl.ds((first + slab) * NZ, NZ), parity, rows]
            return jnp.dot(
                lower.reshape(NZ * WIDTH // PARTS, 2 * WIDTH), solved, preferred_element_type=jnp.float32
            ).reshape(NZ, WIDTH // PARTS, VECS)

        def pass_on(slab, h):
            rows = part_of(h)
            return remote(give.at[slab, :, rows], take.at[slab, :, rows], rs_sems, (level, h, slab), sibling)

        def wide(ref, index):
            return ref[index].astype(jnp.float32)

        def local(slab, h):
            part = terms(slab, c, part_of(h))
            pass_on(slab, h).wait_recv()
            return part + wide(take, (slab, slice(None), part_of(h)))

        def give_all(h):
            for ob in ring_order(mb):
                for oa in ring_order(ma):
                    slab = slab_there(oa, ob)
                    give[slab, :, part_of(h)] = terms(slab, other, part_of(h)).astype(jnp.bfloat16)
                    start(functools.partial(pass_on, slab, h))

        def a_copy(kind, ob, h):
            rows = part_of(h)
            slab = slab_at((2, 2, 1, -1)[kind] % na, ob)
            zs = (low, high, slice(None), slice(None))[kind]
            target = (low_a.at[ob, :, rows], high_a.at[ob, :, rows], near_a.at[0, ob, :, rows], near_a.at[1, ob, :, rows])
            return remote(
                sums.at[slab, zs, rows], target[kind], ra_sems, (level, h, ob, kind), a_peer((1, -1, 1, -1)[kind] % na)
            )

        def b_copy(kind, h):
            rows = part_of(h)
            zs = (low, high, slice(None), slice(None))[kind]
            target = (half_b.at[0, :, rows], half_b.at[1, :, rows], near_b.at[0, :, rows], near_b.at[1, :, rows])
            return remote(
                totals.at[(2, 2, 1, -1)[kind] % nb, zs, rows], target[kind], rb_sems, (level, h, kind),
                b_peer((1, -1, 1, -1)[kind] % nb),
            )

        def joined(value, extra, at_low):
            lower, upper = value[: NZ // 2], value[NZ // 2 :]
            lower, upper = (lower + extra, upper) if at_low else (lower, upper + extra)
            return jnp.concatenate([lower, upper], axis=0)

        def far(h, ob):
            if na > 2:
                sums[slab_at(2, ob), :, part_of(h)] = local(slab_at(2, ob), h).astype(jnp.bfloat16)
                start(lambda: a_copy(0, ob, h))
                start(lambda: a_copy(1, ob, h))

        def near(h, ob):
            rows = part_of(h)
            for kind, oa in ((2, 1), (3, na - 1))[: {1: 0, 2: 1, 4: 2}[na]]:
                value = local(slab_at(oa, ob), h)
                if na > 2:
                    a_copy(kind - 2, ob, h).wait_recv()
                    value = joined(value, wide((low_a, high_a)[kind - 2], (ob, slice(None), rows)), kind == 2)
                sums[slab_at(oa, ob), :, rows] = value.astype(jnp.bfloat16)
                start(functools.partial(a_copy, kind, ob, h))

        def close(h, ob):
            rows = part_of(h)
            value = local(slab_at(0, ob), h)
            for side in range({1: 0, 2: 1, 4: 2}[na]):
                a_copy(2 + side, ob, h).wait_recv()
                value += wide(near_a, (side, ob, slice(None), rows))
            if ob == 0:
                for side in range({1: 0, 2: 1, 4: 2}[nb]):
                    b_copy(2 + side, h).wait_recv()
                    value += wide(near_b, (side, slice(None), rows))
                whole[:, rows] = value
                totals[0, :, rows] = value.astype(jnp.bfloat16)
                for o in range(1, NZ):
                    start(functools.partial(z_copy, o, h))
                return
            if nb > 2 and ob != 2:
                kind = 0 if ob == 1 else 1
                b_copy(kind, h).wait_recv()
                value = joined(value, wide(half_b, (kind, slice(None), rows)), kind == 0)
            totals[ob, :, rows] = value.astype(jnp.bfloat16)
            if nb > 2 and ob == 2:
                start(lambda: b_copy(0, h))
                start(lambda: b_copy(1, h))
            else:
                start(lambda: b_copy(2 if ob == 1 else 3, h))

        def z_copy(o, h):
            rows = part_of(h)
            return remote(
                totals.at[0, (z + o) % NZ, rows], landed.at[o - 1, rows], rz_sems, (level, h, o), z_peer((z + o) % NZ)
            )

        def result(h):
            rows = part_of(h)
            value = whole[z, rows]
            for o in range(1, NZ):
                z_copy(o, h).wait_recv()
                value += wide(landed, (o - 1, rows))
            return value

        return give_all, far, near, close, result, ring_order(nb)

    def step_down(core, level, nx, first, solved, refs, rhs, full, inverse, out):
        sent = []
        give_all, far, near, close, result, order = reduce_steps(core, level, nx, first, solved, refs, sent)
        spread = gather_steps(core, level + 1, nx, full, sent)
        slab = axes_of(core, nx)[2](0, 0)

        def tail(h):
            steps = spread(h)

            def update():
                rows = part_of(h)
                full[slab, z, c, rows] = (rhs[rows] - result(h)).astype(jnp.bfloat16)
                steps[0]()

            return [update, *steps[1:]]

        work = [(h, ob) for h in range(PARTS) for ob in order]
        tails = [tail(h) for h in range(PARTS)]
        for t in range(len(work) + 2):
            if t < len(work):
                h, ob = work[t]
                if ob == order[0]:
                    give_all(h)
                far(h, ob)
            if 1 <= t <= len(work):
                near(*work[t - 1])
            if t >= 2:
                close(*work[t - 2])
            for h in range(PARTS - 1):
                if t > (h + 1) * len(order) + 1 and tails[h]:
                    tails[h].pop(0)()
        while any(tails):
            for steps in tails[::-1]:
                if steps:
                    steps.pop(0)()
        solve(core, level + 1, nx, full, inverse, out)
        for make in sent:
            make().wait_send()

    full_two[y, z, c] = rhs_two[...].astype(jnp.bfloat16)
    pl.semaphore_wait(barrier, len(greeted))

    def top(core):
        sent = []
        spread = gather_steps(core, 0, 1, full_two, sent)
        for step in zip(*[spread(h) for h in range(PARTS)]):
            for part in step:
                part()
        loads[0].wait()
        solve(core, 0, 1, full_two, inv_two, sol_two)
        for make in sent:
            make().wait_send()

    by_core(top)
    y_two = sol_two[...].astype(jnp.bfloat16)

    loads[1].wait()
    loads[2].wait()
    stacked_one = jnp.concatenate([y_two, jnp.zeros_like(y_two)], axis=0)
    by_core(lambda core: step_down(
        core, 0, 2, ROOT_SLABS, stacked_one, level_refs["one"], rhs_one, full_one, inv_one, sol_one
    ))
    y_one = sol_one[...].astype(jnp.bfloat16)

    loads[3].wait()
    stacked_root = jnp.concatenate([y_two, y_one], axis=0)
    by_core(lambda core: step_down(
        core, 1, 4, 0, stacked_root, level_refs["root"], rhs_root, full_root, inv_root, sol_root
    ))


def substitute(rhs_root, rhs_one, rhs_two, inv_root, inv_one, inv_two, placed):
    vmem = pl.BlockSpec(memory_space=pltpu.VMEM)
    hbm = pl.BlockSpec(memory_space=pl.ANY)
    bf16 = jnp.bfloat16

    def planes(*lead):
        return pltpu.VMEM((*lead, WIDTH, VECS), bf16)

    def level(nx):
        return [
            planes(nx * NY, NZ), planes(nx * NY, NZ), planes(nx * NY, NZ),
            planes(NY, NZ // 2), planes(NY, NZ // 2), planes(2, NY, NZ),
            planes(NY, NZ), planes(2, NZ // 2), planes(2, NZ),
            pltpu.VMEM((NZ, WIDTH, VECS), jnp.float32), planes(NZ - 1),
        ]

    sems = pltpu.SemaphoreType.DMA
    out = jax.ShapeDtypeStruct((WIDTH, VECS), jnp.float32)
    return pl.pallas_call(
        main_kernel,
        out_shape=(out, out, out),
        in_specs=[vmem] * 3 + [hbm] * 4,
        out_specs=(vmem,) * 3,
        scratch_shapes=[
            pltpu.VMEM(inv_root.shape, bf16),
            pltpu.VMEM(inv_one.shape, bf16),
            pltpu.VMEM(inv_two.shape, bf16),
            pltpu.VMEM(placed.shape, bf16),
            planes(NY, NZ, NC),
            planes(2 * NY, NZ, NC),
            planes(NX * NY, NZ, NC),
            *level(2),
            *level(4),
            sems((4,)),
            sems((2, 3, PARTS, NZ)),
            sems((2, 3, PARTS, 4)),
            sems((2, 3, PARTS, 4, 4)),
            sems((2, 3, PARTS, NX * NY)),
            sems((2, 2, PARTS, NZ)),
            sems((2, 2, PARTS, 4, 4)),
            sems((2, 2, PARTS, 4)),
            sems((2, 2, PARTS, NX * NY)),
        ],
        compiler_params=pltpu.CompilerParams(
            collective_id=0, has_side_effects=True, vmem_limit_bytes=60 * 2**20
        ),
    )(rhs_root, rhs_one, rhs_two, inv_root, inv_one, inv_two, placed)


def shards(
    rhs_root,
    rhs_one,
    rhs_two,
    inv_root,
    inv_one,
    inv_two,
    lower_one,
    lower_two,
    rows_one,
    rows_two,
    count_one,
    count_two,
):
    span = inv_root.shape[1] + inv_one.shape[1]
    placed = place(rows_two, rows_one, count_two, count_one, lower_two, lower_one, span)
    solved = substitute(rhs_root.T, rhs_one.T, rhs_two.T, inv_root, inv_one, inv_two, placed)
    return tuple(array.T for array in solved)


def solution(mesh):
    cut = P(None, ("leaf", "blk"))
    rows = P(("leaf", "blk"), None)
    return jax.shard_map(
        shards,
        mesh=mesh,
        in_specs=(cut, cut, cut, rows, rows, rows, rows, rows, P(), P(), P(), P()),
        out_specs=(cut, cut, cut),
        check_vma=False,
    )
```

```python
import functools

import jax
import jax.numpy as jnp
from jax import lax
from jax.experimental import pallas as pl
from jax.experimental.pallas import tpu as pltpu
from jax.sharding import PartitionSpec as P

VECS = 128
WIDTH = 64
MESH = pl.DeviceIdType.MESH
NX, NY, NZ, NC = 4, 4, 8, 2
ROOT_SLABS = NX * NY


def main_kernel(
    rhs_root, rhs_one, rhs_two, inv_root_hbm, inv_one_hbm, inv_two_hbm,
    lower_two_hbm, lower_one_hbm, rows_two_hbm, rows_one_hbm, count_two, count_one,
    sol_root, sol_one, sol_two,
    inv_root, inv_one, inv_two, lower, rows_two, rows_one,
    found_two, found_one, index_two, index_one, source_two, source_one, placed_two, placed_one,
    full_two, full_one, full_root, solved, mine, theirs, both,
    *rest,
):
    level_refs = {"one": rest[:6], "root": rest[6:12]}
    local_sems, lower_sems, inv_sems, part_sems, z_sems, a_sems, b_sems, rz_sems, ra_sems, rb_sems = rest[12:]
    leaf = lax.axis_index("leaf")
    blk = lax.axis_index("blk")
    x, y = leaf // NY, leaf % NY
    z, c = blk // NC, blk % NC
    half, pair = x // 2, x % 2
    other = 1 - c
    length = lower_two_hbm.shape[1]

    def z_peer(at):
        return (leaf, at * NC + c)

    sibling = (leaf, z * NC + other)

    inverses = ((inv_two_hbm, inv_two), (inv_one_hbm, inv_one), (inv_root_hbm, inv_root))
    my_rows, their_rows = pl.ds(c * WIDTH, WIDTH), pl.ds(other * WIDTH, WIDTH)
    loads = [
        pltpu.make_async_copy(rows_two_hbm.at[pl.ds(x, 1)], rows_two, local_sems.at[0]),
        pltpu.make_async_copy(rows_one_hbm.at[pl.ds(half, 1)], rows_one, local_sems.at[1]),
        pltpu.make_async_copy(lower_two_hbm, lower.at[0, c], local_sems.at[2]),
        pltpu.make_async_copy(lower_one_hbm, lower.at[1, c], local_sems.at[3]),
        *[
            pltpu.make_async_copy(hbm, inverse.at[my_rows], local_sems.at[4 + level])
            for level, (hbm, inverse) in enumerate(inverses)
        ],
    ]
    for load in loads:
        load.start()

    barrier = pltpu.get_barrier_semaphore()
    greeted = [z_peer((z + o) % NZ) for o in range(1, NZ)]
    greeted += [(x * NY + (y + o) % NY, blk) for o in range(1, NY)]
    greeted += [((x + o) % NX * NY + y, blk) for o in range(1, NX)]
    greeted += [sibling]
    for device in greeted:
        pl.semaphore_signal(barrier, inc=1, device_id=device, device_id_type=MESH)

    def remote(source, target, sems, index, device):
        return pltpu.make_async_remote_copy(
            src_ref=source,
            dst_ref=target,
            send_sem=sems.at[(0, *index)],
            recv_sem=sems.at[(1, *index)],
            device_id=device,
            device_id_type=MESH,
        )

    def axes_of(core, nx):
        mine_x = {1: 0, 2: pair, 4: x}[nx]

        def x_peer(o):
            to = half * 2 + (pair + o) % 2 if nx == 2 else (x + o) % NX
            return (to * NY + y, blk)

        def y_peer(o):
            return (x * NY + (y + o) % NY, blk)

        along_x, along_y = (nx, x_peer), (NY, y_peer)
        first, second = (along_y, along_x) if core == 0 else (along_x, along_y)

        def slab(oa, ob):
            ox, oy = (ob, oa) if core == 0 else (oa, ob)
            return (mine_x + ox) % nx * NY + (y + oy) % NY

        return first, second, slab

    def by_core(body):
        for core in range(NC):
            pl.when(c == core)(functools.partial(body, core))

    lists = (
        (rows_two, count_two, x, found_two, index_two, source_two, placed_two),
        (rows_one, count_one, half, found_one, index_one, source_one, placed_one),
    )

    def index_copy(which):
        return pltpu.make_async_copy(lists[which][3], lists[which][4], local_sems.at[7 + which])

    def invert(which):
        rows, counts, at, found, _, _, placed = lists[which]
        blocks, step = placed.shape[0], 1024
        count = counts[at]

        def body(i, total):
            row = rows[:, pl.ds(pl.multiple_of(i * step, step), step)]
            entry = lax.broadcasted_iota(jnp.int32, (1, step), 1) + i * step + 1
            block = jnp.where(entry <= count, row // 128, -1)
            within = row % 128 - c * WIDTH
            here = lax.broadcasted_iota(jnp.int32, (blocks, step), 0) == block
            mine = lax.broadcasted_iota(jnp.int32, (WIDTH, step), 0) == within
            upper = jnp.where(mine, (entry // 128).astype(jnp.float32), 0.0)
            lower_part = jnp.where(mine, (entry % 128).astype(jnp.float32), 0.0)
            digits = jnp.concatenate([upper, lower_part], axis=0).astype(jnp.bfloat16)
            return total + lax.dot_general(
                jnp.where(here, 1.0, 0.0).astype(jnp.bfloat16), digits, (((1,), (1,)), ((), ())),
                preferred_element_type=jnp.float32,
            )

        total = lax.fori_loop(0, length // step, body, jnp.zeros((blocks, 2 * WIDTH), jnp.float32))
        entry = (total[:, :WIDTH] * 128.0 + total[:, WIDTH:]).astype(jnp.int32)
        found[...] = jnp.clip(jnp.where(entry > 0, entry - 1, length), 0, length)
        index_copy(which).start()

    def lower_copy(which):
        hbm = (lower_two_hbm, lower_one_hbm)[which]
        return remote(hbm, lower.at[which, c], lower_sems, (which,), sibling)

    def lower_arrival(which):
        return remote(lower.at[which, other], lower.at[which, other], lower_sems, (which,), sibling)

    def inverse_copy(level):
        hbm, inverse = inverses[level]
        return remote(hbm, inverse.at[my_rows], inv_sems, (level,), sibling)

    def inverse_here(level):
        inverse = inverses[level][1]
        loads[4 + level].wait()
        remote(inverse.at[their_rows], inverse.at[their_rows], inv_sems, (level,), sibling).wait_recv()

    def turn(which):
        source, step = lists[which][5], 512
        loads[2 + which].wait()
        lower_arrival(which).wait_recv()

        def body(i, carry):
            cols = pl.ds(pl.multiple_of(i * step, step), step)
            both = jnp.concatenate([lower[which, 0, :, cols], lower[which, 1, :, cols]], axis=0)
            source[cols, :] = both.astype(jnp.float32).T
            return carry

        lax.fori_loop(0, length // step, body, 0)
        source[length:, :] = jnp.zeros((source.shape[0] - length, 2 * WIDTH), jnp.float32)

    def fetch(which, start, stop):
        _, _, _, _, index, source, placed = lists[which]

        def body(block, carry):
            picked = [source[pl.ds(index[block, k], 1), :] for k in range(WIDTH)]
            placed[block] = jnp.concatenate(picked, axis=0).astype(jnp.bfloat16)
            return carry

        lax.fori_loop(start, stop, body, 0)

    def fetches(which, start, stop, step):
        return [functools.partial(fetch, which, at, at + step) for at in range(start, stop, step)]

    def run(queue, count):
        for _ in range(min(count, len(queue))):
            queue.pop(0)()

    def gather(core, level, nx, full, out, sent, queue, beside):
        (na, a_peer), (nb, b_peer), slab_at = axes_of(core, nx)
        inverse = inverses[level][1]
        wide = NZ * NC * WIDTH
        ring = na == nb == 4
        low, high, whole = slice(0, NZ // 2), slice(NZ // 2, NZ), slice(0, NZ)

        def start(make):
            make().start()
            sent.append(make)

        def flush():
            while sent:
                sent.pop(0)().wait_send()

        def z_copy(o, arrival=False):
            at = (z + NZ - o) % NZ if arrival else z
            block = full.at[slab_at(0, 0), at, c]
            return remote(block, block, z_sems, (level, o), z_peer((z + o) % NZ))

        def plane(oa, ob, zs=whole):
            return full.at[slab_at(oa, ob), zs, c]

        def a_copy(oa, arrival=False):
            block = plane(na - oa if arrival else 0, 0)
            return remote(block, block, a_sems, (level, oa), a_peer(oa))

        def b_copy(oa, ob, arrival=False):
            block = plane(oa, nb - ob if arrival else 0)
            return remote(block, block, b_sems, (level, oa, ob), b_peer(ob))

        def b_half(oa, kind, arrival=False):
            block = plane(oa, 2 if arrival else (3, 0, 1)[kind], (low, None, high)[kind])
            return remote(block, block, b_sems, (level, oa, kind), b_peer((1, None, 3)[kind]))

        def b_send(oa):
            for ob in (1, 3) if ring else range(1, nb):
                start(functools.partial(b_copy, oa, ob))

        def dot(oa, ob):
            slab = slab_at(oa, ob)
            return jnp.dot(
                inverse[:, pl.ds(pl.multiple_of(slab * wide, wide), wide)],
                full[slab].reshape(wide, VECS),
                preferred_element_type=jnp.float32,
            )

        for o in range(1, NZ):
            start(functools.partial(z_copy, o))
        run(queue, beside[0])
        for o in range(1, NZ):
            z_copy(o, True).wait_recv()
        earlier = len(sent)
        for oa in range(1, na):
            start(functools.partial(a_copy, oa))
        b_send(0)
        for make in [sent.pop(0) for _ in range(earlier)]:
            make().wait_send()
        run(queue, beside[1])
        inverse_here(level)
        total = dot(0, 0)
        for oa in range(1, na):
            a_copy(oa, True).wait_recv()
            b_send(na - oa)
        run(queue, beside[2])
        for oa in range(1, na):
            total += dot(oa, 0)
        for oa in [0, *range(na - 1, 0, -1)]:
            if ring:
                for ob, kind in ((1, 0), (3, 2)):
                    b_copy(oa, ob, True).wait_recv()
                    start(functools.partial(b_half, oa, kind))
            else:
                for ob in range(1, nb):
                    b_copy(oa, ob, True).wait_recv()
            run(queue, beside[3])
            for ob in (1, 3) if ring else range(1, nb):
                total += dot(oa, ob)
        if ring:
            for oa in [0, *range(na - 1, 0, -1)]:
                b_half(oa, 0, True).wait_recv()
                b_half(oa, 2, True).wait_recv()
                total += dot(oa, 2)
        mine[level] = total
        partial = remote(mine.at[level], theirs.at[level], part_sems, (level,), sibling)
        partial.start()
        flush()
        partial.wait()
        total = mine[level] + theirs[level]
        both[...] = total
        out[...] = both[my_rows]
        if level < 2:
            solved[level] = total.astype(jnp.bfloat16)

    def reduce(core, level, nx, terms, refs, sent, queue, beside):
        sums, ra, totals, rb, whole, landed = refs
        (na, a_peer), (nb, b_peer), slab_at = axes_of(core, nx)

        def start(make):
            make().start()
            sent.append(make)

        def a_copy(oa, ob):
            return remote(sums.at[slab_at(oa, ob)], ra.at[oa - 1, ob], ra_sems, (level, oa, ob), a_peer(oa))

        def b_copy(ob):
            return remote(totals.at[ob], rb.at[ob - 1], rb_sems, (level, ob), b_peer(ob))

        def z_copy(o):
            return remote(totals.at[0, (z + o) % NZ], landed.at[o - 1], rz_sems, (level, o), z_peer((z + o) % NZ))

        ring = na == nb == 4
        low, high = slice(0, NZ // 2), slice(NZ // 2, NZ)

        def a_half(kind, ob):
            zs = (low, high)[kind]
            target = ra.at[1, ob, zs]
            return remote(sums.at[slab_at(2, ob), zs], target, ra_sems, (level, 2 * kind, ob), a_peer((1, 3)[kind]))

        order = [*range(1, nb), 0]
        if ring:
            for ob in order:
                slab = slab_at(2, ob)
                sums[slab] = terms(slab).astype(jnp.bfloat16)
                start(functools.partial(a_half, 0, ob))
                start(functools.partial(a_half, 1, ob))
            for ob in order:
                for kind, oa in ((0, 1), (1, 3)):
                    slab = slab_at(oa, ob)
                    value = terms(slab)
                    a_half(kind, ob).wait_recv()
                    zs = (low, high)[kind]
                    extra = ra[1, ob, zs].astype(jnp.float32)
                    halves = [value[: NZ // 2], value[NZ // 2 :]]
                    halves[kind] = halves[kind] + extra
                    sums[slab] = jnp.concatenate(halves, axis=0).astype(jnp.bfloat16)
                    start(functools.partial(a_copy, oa, ob))
        else:
            for ob in order:
                for oa in range(1, na):
                    slab = slab_at(oa, ob)
                    sums[slab] = terms(slab).astype(jnp.bfloat16)
                    start(functools.partial(a_copy, oa, ob))
        run(queue, beside[0])
        for ob in order:
            value = terms(slab_at(0, ob))
            for oa in (1, 3) if ring else range(1, na):
                a_copy(oa, ob).wait_recv()
                value += ra[oa - 1, ob].astype(jnp.float32)
            if ob:
                totals[ob] = value.astype(jnp.bfloat16)
                start(functools.partial(b_copy, ob))
            else:
                whole[...] = value
        run(queue, beside[1])
        value = whole[...]
        for ob in range(1, nb):
            b_copy(ob).wait_recv()
            value += rb[ob - 1].astype(jnp.float32)
        whole[...] = value
        totals[0] = value.astype(jnp.bfloat16)
        for o in range(1, NZ):
            start(functools.partial(z_copy, o))
        run(queue, beside[2])
        value = whole[z]
        for o in range(1, NZ):
            z_copy(o).wait_recv()
            value += landed[o - 1].astype(jnp.float32)
        return value

    def of_two(slab, first):
        blocks = placed_two[pl.ds((first + slab) * NZ, NZ)].reshape(NZ * WIDTH, 2 * WIDTH)
        return jnp.dot(blocks, solved[0], preferred_element_type=jnp.float32)

    def of_one(slab):
        blocks = placed_one[pl.ds(slab * NZ, NZ)].reshape(NZ * WIDTH, 2 * WIDTH)
        return jnp.dot(blocks, solved[1], preferred_element_type=jnp.float32)

    full_two[y, z, c] = rhs_two[...].astype(jnp.bfloat16)
    for full in (full_two, full_one, full_root):
        def blank(slab, carry, full=full):
            full[slab, :, other] = jnp.zeros((NZ, WIDTH, VECS), jnp.bfloat16)
            return carry

        lax.fori_loop(0, full.shape[0], blank, 0)
    pl.semaphore_wait(barrier, len(greeted))
    root_blocks = placed_one.shape[0]

    def start_two():
        lower_copy(0).start()
        inverse_copy(0).start()
        loads[0].wait()
        invert(0)

    def start_one():
        lower_copy(1).start()
        inverse_copy(1).start()
        inverse_copy(2).start()
        loads[1].wait()
        invert(1)

    def wait_index(which):
        index_copy(which).wait()

    def top(core):
        sent = []
        queue = [
            start_two, lambda: turn(0), lambda: wait_index(0),
            *fetches(0, root_blocks, placed_two.shape[0], 16),
        ]
        gather(core, 0, 1, full_two, sol_two, sent, queue, (1, 4, 2, 1))
        run(queue, len(queue))

    by_core(top)

    def middle(core):
        sent = []
        queue = [
            start_one, lambda: turn(1), lambda: wait_index(1),
            *fetches(0, 0, root_blocks, 16), *fetches(1, 0, root_blocks, 16),
        ]
        moved = reduce(
            core, 0, 2, lambda slab: of_two(slab, ROOT_SLABS).reshape(NZ, WIDTH, VECS), level_refs["one"], sent, queue,
            (4, 1, 3),
        )
        full_one[pair * NY + y, z, c] = (rhs_one[...] - moved).astype(jnp.bfloat16)
        gather(core, 1, 2, full_one, sol_one, sent, queue, (3, 2, 1, 1))
        run(queue, len(queue))

    by_core(middle)

    def bottom(core):
        sent = []
        moved = reduce(
            core, 1, 4, lambda slab: (of_two(slab, 0) + of_one(slab)).reshape(NZ, WIDTH, VECS), level_refs["root"],
            sent, [], (0, 0, 0),
        )
        full_root[x * NY + y, z, c] = (rhs_root[...] - moved).astype(jnp.bfloat16)
        gather(core, 2, 4, full_root, sol_root, sent, [], (0, 0, 0, 0))

    by_core(bottom)
    for which in range(2):
        lower_copy(which).wait_send()
    for level in range(3):
        inverse_copy(level).wait_send()


def substitute(rhs_root, rhs_one, rhs_two, inv_root, inv_one, inv_two, lower_two, lower_one, rows_two, rows_one, count_two, count_one):
    vmem = pl.BlockSpec(memory_space=pltpu.VMEM)
    smem = pl.BlockSpec(memory_space=pltpu.SMEM)
    hbm = pl.BlockSpec(memory_space=pl.ANY)
    bf16 = jnp.bfloat16
    length = lower_two.shape[1]
    blocks_one = inv_root.shape[1] // (NC * WIDTH)
    blocks_two = blocks_one + inv_one.shape[1] // (NC * WIDTH)

    def planes(*lead):
        return pltpu.VMEM((*lead, WIDTH, VECS), bf16)

    def level(nx):
        return [
            planes(nx * NY, NZ), planes(3, NY, NZ), planes(NY, NZ), planes(3, NZ),
            pltpu.VMEM((NZ, WIDTH, VECS), jnp.float32), planes(NZ - 1),
        ]

    sems = pltpu.SemaphoreType.DMA
    out = jax.ShapeDtypeStruct((WIDTH, VECS), jnp.float32)
    return pl.pallas_call(
        main_kernel,
        out_shape=(out, out, out),
        in_specs=[vmem] * 3 + [hbm] * 7 + [smem] * 2,
        out_specs=(vmem,) * 3,
        scratch_shapes=[
            *[pltpu.VMEM((2 * WIDTH, inverse.shape[1]), bf16) for inverse in (inv_root, inv_one, inv_two)],
            pltpu.VMEM((2, NC, WIDTH, length), bf16),
            pltpu.VMEM((1, length), jnp.int32),
            pltpu.VMEM((1, length), jnp.int32),
            pltpu.VMEM((blocks_two, WIDTH), jnp.int32),
            pltpu.VMEM((blocks_one, WIDTH), jnp.int32),
            pltpu.SMEM((blocks_two, WIDTH), jnp.int32),
            pltpu.SMEM((blocks_one, WIDTH), jnp.int32),
            pltpu.VMEM((length + 8, 2 * WIDTH), jnp.float32),
            pltpu.VMEM((length + 8, 2 * WIDTH), jnp.float32),
            pltpu.VMEM((blocks_two, WIDTH, 2 * WIDTH), bf16),
            pltpu.VMEM((blocks_one, WIDTH, 2 * WIDTH), bf16),
            planes(NY, NZ, NC),
            planes(2 * NY, NZ, NC),
            planes(NX * NY, NZ, NC),
            pltpu.VMEM((2, 2 * WIDTH, VECS), bf16),
            pltpu.VMEM((3, 2 * WIDTH, VECS), jnp.float32),
            pltpu.VMEM((3, 2 * WIDTH, VECS), jnp.float32),
            pltpu.VMEM((2 * WIDTH, VECS), jnp.float32),
            *level(2),
            *level(4),
            sems((9,)),
            sems((2, 2)),
            sems((2, 3)),
            sems((2, 3)),
            sems((2, 3, NZ)),
            sems((2, 3, 4)),
            sems((2, 3, 4, 4)),
            sems((2, 2, NZ)),
            sems((2, 2, 4, 4)),
            sems((2, 2, 4)),
        ],
        compiler_params=pltpu.CompilerParams(
            collective_id=0, has_side_effects=True, vmem_limit_bytes=60 * 2**20
        ),
    )(rhs_root, rhs_one, rhs_two, inv_root, inv_one, inv_two, lower_two, lower_one, rows_two, rows_one, count_two, count_one)


def hand_over_kernel(*refs):
    for given, out in zip(refs[:3], refs[3:]):
        out[...] = given[...]


def hand_over(arrays):
    vmem = pl.BlockSpec(memory_space=pltpu.VMEM)
    return pl.pallas_call(
        hand_over_kernel,
        out_shape=tuple(jax.ShapeDtypeStruct(array.shape, array.dtype) for array in arrays),
        in_specs=[vmem] * 3,
        out_specs=(vmem,) * 3,
    )(*arrays)


def shards(
    rhs_root,
    rhs_one,
    rhs_two,
    inv_root,
    inv_one,
    inv_two,
    lower_one,
    lower_two,
    rows_one,
    rows_two,
    count_one,
    count_two,
):
    solved = substitute(
        rhs_root.T, rhs_one.T, rhs_two.T, inv_root, inv_one, inv_two,
        lower_two, lower_one, rows_two, rows_one, count_two, count_one,
    )
    return tuple(array.T for array in hand_over(solved))


def solution(mesh):
    cut = P(None, ("leaf", "blk"))
    rows = P(("leaf", "blk"), None)
    return jax.shard_map(
        shards,
        mesh=mesh,
        in_specs=(cut, cut, cut, rows, rows, rows, rows, rows, P(), P(), P(), P()),
        out_specs=(cut, cut, cut),
        check_vma=False,
    )
```

```python
import functools

import jax
import jax.numpy as jnp
from jax import lax
from jax.experimental import pallas as pl
from jax.experimental.pallas import tpu as pltpu
from jax.sharding import PartitionSpec as P

VECS = 128
WIDTH = 64
MESH = pl.DeviceIdType.MESH
NX, NY, NZ, NC = 4, 4, 8, 2
ROOT_SLABS = NX * NY
PARTS = 2


def main_kernel(
    rhs_root, rhs_one, rhs_two, inv_root_hbm, inv_one_hbm, inv_two_hbm,
    lower_two_hbm, lower_one_hbm, rows_two_hbm, rows_one_hbm, count_two, count_one,
    sol_root, sol_one, sol_two,
    inv_root, inv_one, inv_two, lower, rows_two, rows_one,
    found_two, found_one, index_two, index_one, source_two, source_one, placed_two, placed_one,
    full_two, full_one, full_root, solved, mine, theirs, both,
    *rest,
):
    level_refs = {"one": rest[:6], "root": rest[6:12]}
    local_sems, lower_sems, inv_sems, part_sems, z_sems, a_sems, b_sems, rz_sems, ra_sems, rb_sems = rest[12:]
    leaf = lax.axis_index("leaf")
    blk = lax.axis_index("blk")
    x, y = leaf // NY, leaf % NY
    z, c = blk // NC, blk % NC
    half, pair = x // 2, x % 2
    other = 1 - c
    length = lower_two_hbm.shape[1]

    def z_peer(at):
        return (leaf, at * NC + c)

    sibling = (leaf, z * NC + other)

    inverses = ((inv_two_hbm, inv_two), (inv_one_hbm, inv_one), (inv_root_hbm, inv_root))
    my_rows, their_rows = pl.ds(c * WIDTH, WIDTH), pl.ds(other * WIDTH, WIDTH)
    loads = [
        pltpu.make_async_copy(rows_two_hbm.at[pl.ds(x, 1)], rows_two, local_sems.at[0]),
        pltpu.make_async_copy(rows_one_hbm.at[pl.ds(half, 1)], rows_one, local_sems.at[1]),
        pltpu.make_async_copy(lower_two_hbm, lower.at[0, c], local_sems.at[2]),
        pltpu.make_async_copy(lower_one_hbm, lower.at[1, c], local_sems.at[3]),
        *[
            pltpu.make_async_copy(hbm, inverse.at[my_rows], local_sems.at[4 + level])
            for level, (hbm, inverse) in enumerate(inverses)
        ],
    ]
    for load in loads:
        load.start()

    barrier = pltpu.get_barrier_semaphore()
    greeted = [z_peer((z + o) % NZ) for o in range(1, NZ)]
    greeted += [(x * NY + (y + o) % NY, blk) for o in range(1, NY)]
    greeted += [((x + o) % NX * NY + y, blk) for o in range(1, NX)]
    greeted += [sibling]
    for device in greeted:
        pl.semaphore_signal(barrier, inc=1, device_id=device, device_id_type=MESH)

    def remote(source, target, sems, index, device):
        return pltpu.make_async_remote_copy(
            src_ref=source,
            dst_ref=target,
            send_sem=sems.at[(0, *index)],
            recv_sem=sems.at[(1, *index)],
            device_id=device,
            device_id_type=MESH,
        )

    def axes_of(core, nx):
        mine_x = {1: 0, 2: pair, 4: x}[nx]

        def x_peer(o):
            to = half * 2 + (pair + o) % 2 if nx == 2 else (x + o) % NX
            return (to * NY + y, blk)

        def y_peer(o):
            return (x * NY + (y + o) % NY, blk)

        along_x, along_y = (nx, x_peer), (NY, y_peer)
        first, second = (along_y, along_x) if core == 0 else (along_x, along_y)

        def offsets(oa, ob):
            ox, oy = (ob, oa) if core == 0 else (oa, ob)
            return (mine_x + ox) % nx, (y + oy) % NY

        return first, second, offsets

    def by_core(body):
        for core in range(NC):
            pl.when(c == core)(functools.partial(body, core))

    lists = (
        (rows_two, count_two, x, found_two, index_two, source_two, placed_two),
        (rows_one, count_one, half, found_one, index_one, source_one, placed_one),
    )

    def index_copy(which):
        return pltpu.make_async_copy(lists[which][3], lists[which][4], local_sems.at[7 + which])

    def invert(which):
        rows, counts, at, found, _, _, placed = lists[which]
        blocks, step = placed.shape[0], 1024
        count = counts[at]

        def body(i, total):
            row = rows[:, pl.ds(pl.multiple_of(i * step, step), step)]
            entry = lax.broadcasted_iota(jnp.int32, (1, step), 1) + i * step + 1
            block = jnp.where(entry <= count, row // 128, -1)
            within = row % 128 - c * WIDTH
            here = lax.broadcasted_iota(jnp.int32, (blocks, step), 0) == block
            mine = lax.broadcasted_iota(jnp.int32, (WIDTH, step), 0) == within
            upper = jnp.where(mine, (entry // 128).astype(jnp.float32), 0.0)
            lower_part = jnp.where(mine, (entry % 128).astype(jnp.float32), 0.0)
            digits = jnp.concatenate([upper, lower_part], axis=0).astype(jnp.bfloat16)
            return total + lax.dot_general(
                jnp.where(here, 1.0, 0.0).astype(jnp.bfloat16), digits, (((1,), (1,)), ((), ())),
                preferred_element_type=jnp.float32,
            )

        total = lax.fori_loop(0, length // step, body, jnp.zeros((blocks, 2 * WIDTH), jnp.float32))
        entry = (total[:, :WIDTH] * 128.0 + total[:, WIDTH:]).astype(jnp.int32)
        found[...] = jnp.clip(jnp.where(entry > 0, entry - 1, length), 0, length)
        index_copy(which).start()

    def lower_copy(which):
        hbm = (lower_two_hbm, lower_one_hbm)[which]
        return remote(hbm, lower.at[which, c], lower_sems, (which,), sibling)

    def lower_arrival(which):
        return remote(lower.at[which, other], lower.at[which, other], lower_sems, (which,), sibling)

    def inverse_copy(level):
        hbm, inverse = inverses[level]
        return remote(hbm, inverse.at[my_rows], inv_sems, (level,), sibling)

    def inverse_here(level):
        inverse = inverses[level][1]
        loads[4 + level].wait()
        remote(inverse.at[their_rows], inverse.at[their_rows], inv_sems, (level,), sibling).wait_recv()

    def turn(which):
        source, step = lists[which][5], 512
        loads[2 + which].wait()
        lower_arrival(which).wait_recv()

        def body(i, carry):
            cols = pl.ds(pl.multiple_of(i * step, step), step)
            both = jnp.concatenate([lower[which, 0, :, cols], lower[which, 1, :, cols]], axis=0)
            source[cols, :] = both.astype(jnp.float32).T
            return carry

        lax.fori_loop(0, length // step, body, 0)
        source[length:, :] = jnp.zeros((source.shape[0] - length, 2 * WIDTH), jnp.float32)

    def fetch(which, start, stop):
        _, _, _, _, index, source, placed = lists[which]

        def body(block, carry):
            picked = [source[pl.ds(index[block, k], 1), :] for k in range(WIDTH)]
            placed[block] = jnp.concatenate(picked, axis=0).astype(jnp.bfloat16)
            return carry

        lax.fori_loop(start, stop, body, 0)

    def fetches(which, start, stop, step):
        return [functools.partial(fetch, which, at, at + step) for at in range(start, stop, step)]

    def run(queue, count):
        for _ in range(min(count, len(queue))):
            queue.pop(0)()

    def part_of(h):
        return slice(h * WIDTH // PARTS, (h + 1) * WIDTH // PARTS)

    def started(sent, make):
        make().start()
        sent.append(make)

    def flush(sent):
        while sent:
            sent.pop(0)().wait_send()

    def product(level, full, at_x, at_y):
        wide = NZ * NC * WIDTH
        slab = at_x * NY + at_y
        return jnp.dot(
            inverses[level][1][:, pl.ds(pl.multiple_of(slab * wide, wide), wide)],
            full[at_x, at_y].reshape(wide, VECS),
            preferred_element_type=jnp.float32,
        )

    def conclude(level, total, out, sent):
        mine[level] = total
        partial = remote(mine.at[level], theirs.at[level], part_sems, (level,), sibling)
        partial.start()
        flush(sent)
        partial.wait()
        total = mine[level] + theirs[level]
        both[...] = total
        out[...] = both[my_rows]
        if level < 2:
            solved[level] = total.astype(jnp.bfloat16)

    def top(core):
        sent = []

        def z_copy(o, arrival=False):
            at = (z + NZ - o) % NZ if arrival else z
            block = full_two.at[0, y, at, c] if core == 0 else full_two.at[0, :, at, c]
            return remote(block, block, z_sems, (0, 0, o), z_peer((z + o) % NZ))

        def y_copy(o, arrival=False):
            at = (y + NY - o) % NY if arrival else y
            block = full_two.at[0, at, :, c] if core == 0 else full_two.at[0, at, z, c]
            return remote(block, block, a_sems, (0, 0, o), (x * NY + (y + o) % NY, blk))

        near, far = ((z_copy, NZ), (y_copy, NY))[:: 1 if core == 0 else -1]
        for o in range(1, near[1]):
            started(sent, functools.partial(near[0], o))
        start_two()
        for o in range(1, near[1]):
            near[0](o, True).wait_recv()
        for o in range(1, far[1]):
            started(sent, functools.partial(far[0], o))
        turn(0)
        wait_index(0)
        fetch(0, root_blocks, placed_two.shape[0])
        inverse_here(0)
        for o in range(1, far[1]):
            far[0](o, True).wait_recv()
        total = jnp.zeros((2 * WIDTH, VECS), jnp.float32)
        for at_y in range(NY):
            total += product(0, full_two, 0, at_y)
        conclude(0, total, sol_two, sent)

    def level_down(level, nx, terms, refs, rhs, full, out, queue, beside):
        sums, ra, totals, rb, whole, landed = refs
        sent, last = [], []
        plan = [axes_of(h, nx) for h in range(PARTS)]
        ring = nx == 4
        low, high, every = slice(0, NZ // 2), slice(NZ // 2, NZ), slice(None)

        def a_copy(h, oa, zs, target, to):
            (_, a_peer), (nb, _), _ = plan[h]
            at = (slice(0, nb), zs, part_of(h))
            return remote(
                sums.at[(oa - 1, *at)], ra.at[(target - 1, *at)], ra_sems,
                (level, h, oa, {low: 0, high: 1, every: 0}[zs]), a_peer(to),
            )

        def b_copy(ob, h):
            return remote(
                totals.at[ob, :, part_of(h)], rb.at[ob - 1, :, part_of(h)], rb_sems, (level, h, ob), plan[h][1][1](ob)
            )

        def z_copy(o, h):
            return remote(
                totals.at[0, (z + o) % NZ, part_of(h)], landed.at[o - 1, part_of(h)], rz_sems, (level, h, o),
                z_peer((z + o) % NZ),
            )

        def make(h, oa):
            for ob in range(plan[h][1][0]):
                sums[oa - 1, ob, :, part_of(h)] = terms(plan[h][2](oa, ob), part_of(h)).astype(jnp.bfloat16)

        def a_start():
            if not ring:
                for h in range(PARTS):
                    for oa in range(1, plan[h][0][0]):
                        make(h, oa)
                        started(sent, functools.partial(a_copy, h, oa, every, oa, oa))
                return
            for h in range(PARTS):
                make(h, 2)
                started(sent, functools.partial(a_copy, h, 2, low, 2, 1))
                started(sent, functools.partial(a_copy, h, 2, high, 2, 3))
            for h in range(PARTS):
                for oa, zs in ((1, high), (3, low)):
                    make(h, oa)
                    started(sent, functools.partial(a_copy, h, oa, zs, oa, oa))

        def a_middle(h):
            if ring:
                for oa, zs, to in ((1, low, 1), (3, high, 3)):
                    a_copy(h, 2, zs, 2, to).wait_recv()
                    at = (slice(0, NY), zs, part_of(h))
                    joined = sums[(oa - 1, *at)].astype(jnp.float32) + ra[(1, *at)].astype(jnp.float32)
                    sums[(oa - 1, *at)] = joined.astype(jnp.bfloat16)
                    started(sent, functools.partial(a_copy, h, oa, zs, oa, oa))

        def a_close(h):
            (na, _), (nb, _), offsets = plan[h]
            rows = part_of(h)
            for oa in (1, 3) if ring else range(1, na):
                for zs in (low, high) if ring else (every,):
                    a_copy(h, oa, zs, oa, oa).wait_recv()
            for ob in [*range(1, nb), 0]:
                value = terms(offsets(0, ob), rows)
                for oa in (1, 3) if ring else range(1, na):
                    value += ra[oa - 1, ob, :, rows].astype(jnp.float32)
                if ob:
                    totals[ob, :, rows] = value.astype(jnp.bfloat16)
                    started(sent, functools.partial(b_copy, ob, h))
                else:
                    whole[:, rows] = value

        def b_close(h):
            rows = part_of(h)
            value = whole[:, rows]
            for ob in range(1, plan[h][1][0]):
                b_copy(ob, h).wait_recv()
                value += rb[ob - 1, :, rows].astype(jnp.float32)
            whole[:, rows] = value
            totals[0, :, rows] = value.astype(jnp.bfloat16)
            for o in range(1, NZ):
                started(sent, functools.partial(z_copy, o, h))

        def z_close(h):
            rows = part_of(h)
            value = whole[z, rows]
            for o in range(1, NZ):
                z_copy(o, h).wait_recv()
                value += landed[o - 1, rows].astype(jnp.float32)
            at_x, at_y = plan[h][2](0, 0)
            full[at_x, at_y, z, c, rows] = (rhs[rows] - value).astype(jnp.bfloat16)
            for o in range(1, NZ):
                started(sent, functools.partial(own_copy, o, h))

        def own_copy(o, h, arrival=False):
            at = (z + NZ - o) % NZ if arrival else z
            block = full.at[(*plan[h][2](0, 0), at, c, part_of(h))]
            return remote(block, block, z_sems, (level + 1, h, o), z_peer((z + o) % NZ))

        def near_copy(oa, h, arrival=False):
            (na, a_peer), _, offsets = plan[h]
            block = full.at[(*offsets(na - oa if arrival else 0, 0), every, c, part_of(h))]
            return remote(block, block, a_sems, (level + 1, h, oa), a_peer(oa))

        def far_copy(h, origin, zs, to):
            (_, b_peer), offsets = plan[h][1:]
            at_x, at_y = offsets(0, origin)
            line = (at_x, every) if h == 0 else (every, at_y)
            block = full.at[(*line, zs, c, part_of(h))]
            kind = to if origin == 0 else 2
            return remote(
                block, block, b_sems, (level + 1, h, kind, {low: 0, high: 1, every: 0}[zs]), b_peer(to)
            )

        def far_arrival(h, ob, zs, by):
            (nb, b_peer), offsets = plan[h][1:]
            at_x, at_y = offsets(0, ob)
            line = (at_x, every) if h == 0 else (every, at_y)
            block = full.at[(*line, zs, c, part_of(h))]
            return remote(block, block, b_sems, (level + 1, h, by, {low: 0, high: 1, every: 0}[zs]), b_peer(0 if nb < 2 else 1))

        def near_start(h):
            for o in range(1, NZ):
                own_copy(o, h, True).wait_recv()
            for oa in range(1, plan[h][0][0]):
                started(sent, functools.partial(near_copy, oa, h))

        def far_start(h):
            for oa in range(1, plan[h][0][0]):
                near_copy(oa, h, True).wait_recv()
            if ring:
                for to, zs in ((1, low), (3, high), (1, high), (3, low)):
                    started(last, functools.partial(far_copy, h, 0, zs, to))
            else:
                for ob in range(1, plan[h][1][0]):
                    started(last, functools.partial(far_copy, h, 0, every, ob))

        def far_middle(h):
            if ring:
                for origin, zs, to in ((3, low, 1), (1, high, 3)):
                    far_arrival(h, origin, zs, to).wait_recv()
                    started(last, functools.partial(far_copy, h, origin, zs, to))

        both_parts = range(PARTS)
        a_start()
        run(queue, beside[0])
        for h in both_parts:
            a_middle(h)
        run(queue, beside[1])
        for h in both_parts:
            a_close(h)
        run(queue, beside[2])
        for h in both_parts:
            b_close(h)
        run(queue, beside[3])
        for h in both_parts:
            z_close(h)
        run(queue, beside[4])
        for h in both_parts:
            near_start(h)
        run(queue, beside[5])
        for h in both_parts:
            far_start(h)
        run(queue, beside[6])
        for h in both_parts:
            far_middle(h)
        run(queue, len(queue))
        flush(sent)
        inverse_here(level + 1)
        total = jnp.zeros((2 * WIDTH, VECS), jnp.float32)

        def products(total, at):
            for ox, oy in at:
                total += product(level + 1, full, *plan[0][2](oy, ox))
            return total

        if ring:
            for h in both_parts:
                far_arrival(h, 3, high, 1).wait_recv()
                far_arrival(h, 1, low, 3).wait_recv()
            total = products(total, [(ox, oy) for ox in (0, 1, 3) for oy in (0, 1, 3)])
            for h in both_parts:
                far_arrival(h, 2, low, 2).wait_recv()
                far_arrival(h, 2, high, 2).wait_recv()
            total = products(total, [(ox, oy) for ox in range(4) for oy in range(4) if 2 in (ox, oy)])
        else:
            for h in both_parts:
                nb = plan[h][1][0]
                for ob in range(1, nb):
                    far_arrival(h, nb - ob, every, ob).wait_recv()
            total = products(total, [(ox, oy) for ox in range(nx) for oy in range(NY)])
        conclude(level + 1, total, out, last)

    def of_list(placed, which, first, at, rows):
        blocks = placed[pl.ds((first + at[0] * NY + at[1]) * NZ, NZ), rows]
        return jnp.dot(
            blocks.reshape(-1, 2 * WIDTH), solved[which], preferred_element_type=jnp.float32
        ).reshape(*blocks.shape[:2], VECS)

    full_two[0, y, z, c] = rhs_two[...].astype(jnp.bfloat16)
    for full in (full_two, full_one, full_root):
        def blank(slab, carry, full=full):
            full[slab // NY, slab % NY, :, other] = jnp.zeros((NZ, WIDTH, VECS), jnp.bfloat16)
            return carry

        lax.fori_loop(0, full.shape[0] * NY, blank, 0)
    pl.semaphore_wait(barrier, len(greeted))
    root_blocks = placed_one.shape[0]

    def start_two():
        lower_copy(0).start()
        inverse_copy(0).start()
        loads[0].wait()
        invert(0)

    def start_one():
        lower_copy(1).start()
        inverse_copy(1).start()
        inverse_copy(2).start()
        loads[1].wait()
        invert(1)

    def wait_index(which):
        index_copy(which).wait()

    by_core(top)

    queue = [
        start_one, lambda: turn(1), *fetches(0, 0, root_blocks, 16), lambda: wait_index(1),
        *fetches(1, 0, root_blocks, 16),
    ]
    level_down(
        0, 2, lambda at, rows: of_list(placed_two, 0, ROOT_SLABS, at, rows), level_refs["one"],
        rhs_one, full_one, sol_one, queue, (3, 0, 2, 3, 3, 2, 2),
    )

    level_down(
        1, 4, lambda at, rows: of_list(placed_two, 0, 0, at, rows) + of_list(placed_one, 1, 0, at, rows),
        level_refs["root"], rhs_root, full_root, sol_root, [], (0,) * 7,
    )
    for which in range(2):
        lower_copy(which).wait_send()
    for level in range(3):
        inverse_copy(level).wait_send()


def substitute(rhs_root, rhs_one, rhs_two, inv_root, inv_one, inv_two, lower_two, lower_one, rows_two, rows_one, count_two, count_one):
    vmem = pl.BlockSpec(memory_space=pltpu.VMEM)
    smem = pl.BlockSpec(memory_space=pltpu.SMEM)
    hbm = pl.BlockSpec(memory_space=pl.ANY)
    bf16 = jnp.bfloat16
    length = lower_two.shape[1]
    blocks_one = inv_root.shape[1] // (NC * WIDTH)
    blocks_two = blocks_one + inv_one.shape[1] // (NC * WIDTH)

    def planes(*lead):
        return pltpu.VMEM((*lead, WIDTH, VECS), bf16)

    def level(nx):
        return [
            planes(3, NY, NZ), planes(3, NY, NZ), planes(NY, NZ), planes(3, NZ),
            pltpu.VMEM((NZ, WIDTH, VECS), jnp.float32), planes(NZ - 1),
        ]

    sems = pltpu.SemaphoreType.DMA
    out = jax.ShapeDtypeStruct((WIDTH, VECS), jnp.float32)
    return pl.pallas_call(
        main_kernel,
        out_shape=(out, out, out),
        in_specs=[vmem] * 3 + [hbm] * 7 + [smem] * 2,
        out_specs=(vmem,) * 3,
        scratch_shapes=[
            *[pltpu.VMEM((2 * WIDTH, inverse.shape[1]), bf16) for inverse in (inv_root, inv_one, inv_two)],
            pltpu.VMEM((2, NC, WIDTH, length), bf16),
            pltpu.VMEM((1, length), jnp.int32),
            pltpu.VMEM((1, length), jnp.int32),
            pltpu.VMEM((blocks_two, WIDTH), jnp.int32),
            pltpu.VMEM((blocks_one, WIDTH), jnp.int32),
            pltpu.SMEM((blocks_two, WIDTH), jnp.int32),
            pltpu.SMEM((blocks_one, WIDTH), jnp.int32),
            pltpu.VMEM((length + 8, 2 * WIDTH), jnp.float32),
            pltpu.VMEM((length + 8, 2 * WIDTH), jnp.float32),
            pltpu.VMEM((blocks_two, WIDTH, 2 * WIDTH), bf16),
            pltpu.VMEM((blocks_one, WIDTH, 2 * WIDTH), bf16),
            planes(1, NY, NZ, NC),
            planes(2, NY, NZ, NC),
            planes(NX, NY, NZ, NC),
            pltpu.VMEM((2, 2 * WIDTH, VECS), bf16),
            pltpu.VMEM((3, 2 * WIDTH, VECS), jnp.float32),
            pltpu.VMEM((3, 2 * WIDTH, VECS), jnp.float32),
            pltpu.VMEM((2 * WIDTH, VECS), jnp.float32),
            *level(2),
            *level(4),
            sems((9,)),
            sems((2, 2)),
            sems((2, 3)),
            sems((2, 3)),
            sems((2, 3, PARTS, NZ)),
            sems((2, 3, PARTS, 4)),
            sems((2, 3, PARTS, 4, 2)),
            sems((2, 2, PARTS, NZ)),
            sems((2, 2, PARTS, 4, 2)),
            sems((2, 2, PARTS, 4)),
        ],
        compiler_params=pltpu.CompilerParams(
            collective_id=0, has_side_effects=True, vmem_limit_bytes=60 * 2**20
        ),
    )(rhs_root, rhs_one, rhs_two, inv_root, inv_one, inv_two, lower_two, lower_one, rows_two, rows_one, count_two, count_one)


def hand_over_kernel(*refs):
    for given, out in zip(refs[:3], refs[3:]):
        out[...] = given[...]


def hand_over(arrays):
    vmem = pl.BlockSpec(memory_space=pltpu.VMEM)
    return pl.pallas_call(
        hand_over_kernel,
        out_shape=tuple(jax.ShapeDtypeStruct(array.shape, array.dtype) for array in arrays),
        in_specs=[vmem] * 3,
        out_specs=(vmem,) * 3,
    )(*arrays)


def shards(
    rhs_root,
    rhs_one,
    rhs_two,
    inv_root,
    inv_one,
    inv_two,
    lower_one,
    lower_two,
    rows_one,
    rows_two,
    count_one,
    count_two,
):
    solved = substitute(
        rhs_root.T, rhs_one.T, rhs_two.T, inv_root, inv_one, inv_two,
        lower_two, lower_one, rows_two, rows_one, count_two, count_one,
    )
    return tuple(array.T for array in hand_over(solved))


def solution(mesh):
    cut = P(None, ("leaf", "blk"))
    rows = P(("leaf", "blk"), None)
    return jax.shard_map(
        shards,
        mesh=mesh,
        in_specs=(cut, cut, cut, rows, rows, rows, rows, rows, P(), P(), P(), P()),
        out_specs=(cut, cut, cut),
        check_vma=False,
    )
```

```python
import functools

import jax
import jax.numpy as jnp
from jax import lax
from jax.experimental import pallas as pl
from jax.experimental.pallas import tpu as pltpu
from jax.sharding import PartitionSpec as P

VECS = 128
WIDTH = 64
MESH = pl.DeviceIdType.MESH
NX, NY, NZ, NC = 4, 4, 8, 2
ROOT_SLABS = NX * NY
PARTS = 4
FAR_FIRST = (4, 3, 5, 2, 6, 1, 7)
TOP_ROWS = 48


def main_kernel(
    rhs_root, rhs_one, rhs_two, inv_root_hbm, inv_one_hbm, inv_two_hbm,
    lower_two_hbm, lower_one_hbm, rows_two_hbm, rows_one_hbm, count_two, count_one,
    sol_root, sol_one, sol_two,
    inv_root, inv_one, inv_two, lower, rows_two, rows_one,
    found_two, found_one, index_two, index_one, source_two, source_one, placed_two, placed_one,
    full_two, full_one, full_root, solved, mine, theirs, both,
    *rest,
):
    level_refs = {"one": rest[:6], "root": rest[6:12]}
    local_sems, lower_sems, inv_sems, part_sems, z_sems, a_sems, b_sems, rz_sems, ra_sems, rb_sems = rest[12:]
    leaf = lax.axis_index("leaf")
    blk = lax.axis_index("blk")
    x, y = leaf // NY, leaf % NY
    z, c = blk // NC, blk % NC
    half, pair = x // 2, x % 2
    other = 1 - c
    length = lower_two_hbm.shape[1]

    def z_peer(at):
        return (leaf, at * NC + c)

    sibling = (leaf, z * NC + other)

    inverses = ((inv_two_hbm, inv_two), (inv_one_hbm, inv_one), (inv_root_hbm, inv_root))
    my_rows, their_rows = pl.ds(c * WIDTH, WIDTH), pl.ds(other * WIDTH, WIDTH)
    loads = [
        pltpu.make_async_copy(rows_two_hbm.at[pl.ds(x, 1)], rows_two, local_sems.at[0]),
        pltpu.make_async_copy(rows_one_hbm.at[pl.ds(half, 1)], rows_one, local_sems.at[1]),
        pltpu.make_async_copy(lower_two_hbm, lower.at[0, c], local_sems.at[2]),
        pltpu.make_async_copy(lower_one_hbm, lower.at[1, c], local_sems.at[3]),
        *[
            pltpu.make_async_copy(hbm, inverse.at[my_rows], local_sems.at[4 + level])
            for level, (hbm, inverse) in enumerate(inverses)
        ],
    ]
    for load in loads:
        load.start()

    barrier = pltpu.get_barrier_semaphore()
    greeted = [z_peer((z + o) % NZ) for o in range(1, NZ)]
    greeted += [(x * NY + (y + o) % NY, blk) for o in range(1, NY)]
    greeted += [((x + o) % NX * NY + y, blk) for o in range(1, NX)]
    greeted += [sibling]
    for device in greeted:
        pl.semaphore_signal(barrier, inc=1, device_id=device, device_id_type=MESH)

    def remote(source, target, sems, index, device):
        return pltpu.make_async_remote_copy(
            src_ref=source,
            dst_ref=target,
            send_sem=sems.at[(0, *index)],
            recv_sem=sems.at[(1, *index)],
            device_id=device,
            device_id_type=MESH,
        )

    def axes_of(core, nx):
        mine_x = {1: 0, 2: pair, 4: x}[nx]

        def x_peer(o):
            to = half * 2 + (pair + o) % 2 if nx == 2 else (x + o) % NX
            return (to * NY + y, blk)

        def y_peer(o):
            return (x * NY + (y + o) % NY, blk)

        along_x, along_y = (nx, x_peer), (NY, y_peer)
        first, second = (along_y, along_x) if core == 0 else (along_x, along_y)

        def offsets(oa, ob):
            ox, oy = (ob, oa) if core == 0 else (oa, ob)
            return (mine_x + ox) % nx, (y + oy) % NY

        return first, second, offsets

    lists = (
        (rows_two, count_two, x, found_two, index_two, source_two, placed_two),
        (rows_one, count_one, half, found_one, index_one, source_one, placed_one),
    )

    def index_copy(which):
        return pltpu.make_async_copy(lists[which][3], lists[which][4], local_sems.at[7 + which])

    def invert(which):
        rows, counts, at, found, _, _, placed = lists[which]
        blocks, step = placed.shape[0], 1024
        count = counts[at]

        def body(i, total):
            row = rows[:, pl.ds(pl.multiple_of(i * step, step), step)]
            entry = lax.broadcasted_iota(jnp.int32, (1, step), 1) + i * step + 1
            block = jnp.where(entry <= count, row // 128, -1)
            within = row % 128 - c * WIDTH
            here = lax.broadcasted_iota(jnp.int32, (blocks, step), 0) == block
            mine = lax.broadcasted_iota(jnp.int32, (WIDTH, step), 0) == within
            upper = jnp.where(mine, (entry // 128).astype(jnp.float32), 0.0)
            lower_part = jnp.where(mine, (entry % 128).astype(jnp.float32), 0.0)
            digits = jnp.concatenate([upper, lower_part], axis=0).astype(jnp.bfloat16)
            return total + lax.dot_general(
                jnp.where(here, 1.0, 0.0).astype(jnp.bfloat16), digits, (((1,), (1,)), ((), ())),
                preferred_element_type=jnp.float32,
            )

        total = lax.fori_loop(0, length // step, body, jnp.zeros((blocks, 2 * WIDTH), jnp.float32))
        entry = (total[:, :WIDTH] * 128.0 + total[:, WIDTH:]).astype(jnp.int32)
        found[...] = jnp.clip(jnp.where(entry > 0, entry - 1, length), 0, length)
        index_copy(which).start()

    def lower_copy(which):
        hbm = (lower_two_hbm, lower_one_hbm)[which]
        return remote(hbm, lower.at[which, c], lower_sems, (which,), sibling)

    def lower_arrival(which):
        return remote(lower.at[which, other], lower.at[which, other], lower_sems, (which,), sibling)

    def inverse_copy(level):
        hbm, inverse = inverses[level]
        return remote(hbm, inverse.at[my_rows], inv_sems, (level,), sibling)

    def inverse_here(level):
        inverse = inverses[level][1]
        loads[4 + level].wait()
        remote(inverse.at[their_rows], inverse.at[their_rows], inv_sems, (level,), sibling).wait_recv()

    def turn(which):
        source, step = lists[which][5], 512
        loads[2 + which].wait()
        lower_arrival(which).wait_recv()

        def body(i, carry):
            cols = pl.ds(pl.multiple_of(i * step, step), step)
            both = jnp.concatenate([lower[which, 0, :, cols], lower[which, 1, :, cols]], axis=0)
            source[cols, :] = both.astype(jnp.float32).T
            return carry

        lax.fori_loop(0, length // step, body, 0)
        source[length:, :] = jnp.zeros((source.shape[0] - length, 2 * WIDTH), jnp.float32)

    def fetch(which, start, stop):
        _, _, _, _, index, source, placed = lists[which]

        def body(block, carry):
            picked = [source[pl.ds(index[block, k], 1), :] for k in range(WIDTH)]
            placed[block] = jnp.concatenate(picked, axis=0).astype(jnp.bfloat16)
            return carry

        lax.fori_loop(start, stop, body, 0)

    def fetches(which, start, stop, step):
        return [functools.partial(fetch, which, at, at + step) for at in range(start, stop, step)]

    def run(queue, count):
        for _ in range(min(count, len(queue))):
            queue.pop(0)()

    def blank(full):
        def body(slab, carry):
            full[slab // NY, slab % NY, :, other] = jnp.zeros((NZ, WIDTH, VECS), jnp.bfloat16)
            return carry

        lax.fori_loop(0, full.shape[0] * NY, body, 0)

    def part_of(h):
        return slice(h * WIDTH // PARTS, (h + 1) * WIDTH // PARTS)

    def started(sent, make):
        make().start()
        sent.append(make)

    def flush(sent):
        while sent:
            sent.pop(0)().wait_send()

    def product(level, full, at_x, at_y):
        wide = NZ * NC * WIDTH
        slab = at_x * NY + at_y
        return jnp.dot(
            inverses[level][1][:, pl.ds(pl.multiple_of(slab * wide, wide), wide)],
            full[at_x, at_y].reshape(wide, VECS),
            preferred_element_type=jnp.float32,
        )

    def conclude(level, total, out, sent):
        mine[level] = total
        partial = remote(mine.at[level], theirs.at[level], part_sems, (level,), sibling)
        partial.start()
        flush(sent)
        partial.wait()
        total = mine[level] + theirs[level]
        both[...] = total
        out[...] = both[my_rows]
        if level < 2:
            solved[level] = total.astype(jnp.bfloat16)

    def top():
        sent = []
        rows = (slice(0, TOP_ROWS), slice(TOP_ROWS, WIDTH))

        def z_copy(h, o, arrival=False):
            at = (z + NZ - o) % NZ if arrival else z
            block = full_two.at[0, slice(None) if h else y, at, c, rows[h]]
            return remote(block, block, z_sems, (0, h, o), z_peer((z + o) % NZ))

        def y_copy(h, o, arrival=False):
            at = (y + NY - o) % NY if arrival else y
            block = full_two.at[0, at, z if h else slice(None), c, rows[h]]
            return remote(block, block, a_sems, (0, h, o), (x * NY + (y + o) % NY, blk))

        along_z = lambda h: [functools.partial(z_copy, h, o) for o in FAR_FIRST]
        along_y = lambda h: [functools.partial(y_copy, h, o) for o in range(1, NY)]
        for make in along_y(1) + along_z(0):
            started(sent, make)
        start_two()
        for first, second in ((along_y(1), along_z(1)), (along_z(0), along_y(0))):
            for make in first:
                make(True).wait_recv()
            for make in second:
                started(sent, make)
        blank(full_one)
        blank(full_root)
        turn(0)
        wait_index(0)
        fetch(0, root_blocks, placed_two.shape[0])
        inverse_here(0)
        for make in along_y(0) + along_z(1):
            make(True).wait_recv()
        total = jnp.zeros((2 * WIDTH, VECS), jnp.float32)
        for at_y in range(NY):
            total += product(0, full_two, 0, at_y)
        conclude(0, total, sol_two, sent)

    def level_down(level, nx, terms, refs, rhs, full, out, queue, beside):
        sums, ra, totals, rb, whole, landed = refs
        sent, last = [], []
        plan = [axes_of(h % 2, nx) for h in range(PARTS)]
        ring = nx == 4
        low, high, every = slice(0, NZ // 2), slice(NZ // 2, NZ), slice(None)

        def a_copy(h, oa, zs, target, to):
            (_, a_peer), (nb, _), _ = plan[h]
            at = (slice(0, nb), zs, part_of(h))
            return remote(
                sums.at[(oa - 1, *at)], ra.at[(target - 1, *at)], ra_sems,
                (level, h, oa, {low: 0, high: 1, every: 0}[zs]), a_peer(to),
            )

        def b_copy(ob, h):
            return remote(
                totals.at[ob, :, part_of(h)], rb.at[ob - 1, :, part_of(h)], rb_sems, (level, h, ob), plan[h][1][1](ob)
            )

        def z_copy(o, h):
            return remote(
                totals.at[0, (z + o) % NZ, part_of(h)], landed.at[o - 1, part_of(h)], rz_sems, (level, h, o),
                z_peer((z + o) % NZ),
            )

        def make(h, oa):
            for ob in range(plan[h][1][0]):
                sums[oa - 1, ob, :, part_of(h)] = terms(plan[h][2](oa, ob), part_of(h)).astype(jnp.bfloat16)

        def a_start():
            if not ring:
                for h in range(PARTS):
                    for oa in range(1, plan[h][0][0]):
                        make(h, oa)
                        started(sent, functools.partial(a_copy, h, oa, every, oa, oa))
                return
            for h in range(PARTS):
                make(h, 2)
                started(sent, functools.partial(a_copy, h, 2, low, 2, 1))
                started(sent, functools.partial(a_copy, h, 2, high, 2, 3))
            for h in range(PARTS):
                for oa, zs in ((1, high), (3, low)):
                    make(h, oa)
                    started(sent, functools.partial(a_copy, h, oa, zs, oa, oa))

        def a_middle(h):
            if ring:
                for oa, zs, to in ((1, low, 1), (3, high, 3)):
                    a_copy(h, 2, zs, 2, to).wait_recv()
                    at = (slice(0, NY), zs, part_of(h))
                    joined = sums[(oa - 1, *at)].astype(jnp.float32) + ra[(1, *at)].astype(jnp.float32)
                    sums[(oa - 1, *at)] = joined.astype(jnp.bfloat16)
                    started(sent, functools.partial(a_copy, h, oa, zs, oa, oa))

        def a_close(h):
            (na, _), (nb, _), offsets = plan[h]
            rows = part_of(h)
            for oa in (1, 3) if ring else range(1, na):
                for zs in (low, high) if ring else (every,):
                    a_copy(h, oa, zs, oa, oa).wait_recv()
            for ob in [*range(1, nb), 0]:
                value = terms(offsets(0, ob), rows)
                for oa in (1, 3) if ring else range(1, na):
                    value += ra[oa - 1, ob, :, rows].astype(jnp.float32)
                if ob:
                    totals[ob, :, rows] = value.astype(jnp.bfloat16)
                    started(sent, functools.partial(b_copy, ob, h))
                else:
                    whole[:, rows] = value

        def b_close(h):
            rows = part_of(h)
            value = whole[:, rows]
            for ob in range(1, plan[h][1][0]):
                b_copy(ob, h).wait_recv()
                value += rb[ob - 1, :, rows].astype(jnp.float32)
            whole[:, rows] = value
            totals[0, :, rows] = value.astype(jnp.bfloat16)
            for o in FAR_FIRST:
                started(sent, functools.partial(z_copy, o, h))

        def z_close(h):
            rows = part_of(h)
            value = whole[z, rows]
            for o in range(1, NZ):
                z_copy(o, h).wait_recv()
                value += landed[o - 1, rows].astype(jnp.float32)
            at_x, at_y = plan[h][2](0, 0)
            full[at_x, at_y, z, c, rows] = (rhs[rows] - value).astype(jnp.bfloat16)
            for o in FAR_FIRST:
                started(sent, functools.partial(own_copy, o, h))

        def own_copy(o, h, arrival=False):
            at = (z + NZ - o) % NZ if arrival else z
            block = full.at[(*plan[h][2](0, 0), at, c, part_of(h))]
            return remote(block, block, z_sems, (level + 1, h, o), z_peer((z + o) % NZ))

        def near_copy(oa, h, arrival=False):
            (na, a_peer), _, offsets = plan[h]
            block = full.at[(*offsets(na - oa if arrival else 0, 0), every, c, part_of(h))]
            return remote(block, block, a_sems, (level + 1, h, oa), a_peer(oa))

        def far_copy(h, origin, zs, to):
            (_, b_peer), offsets = plan[h][1:]
            at_x, at_y = offsets(0, origin)
            line = (at_x, every) if h % 2 == 0 else (every, at_y)
            block = full.at[(*line, zs, c, part_of(h))]
            kind = to if origin == 0 else 2
            return remote(
                block, block, b_sems, (level + 1, h, kind, {low: 0, high: 1, every: 0}[zs]), b_peer(to)
            )

        def far_arrival(h, ob, zs, by):
            (nb, b_peer), offsets = plan[h][1:]
            at_x, at_y = offsets(0, ob)
            line = (at_x, every) if h % 2 == 0 else (every, at_y)
            block = full.at[(*line, zs, c, part_of(h))]
            return remote(block, block, b_sems, (level + 1, h, by, {low: 0, high: 1, every: 0}[zs]), b_peer(0 if nb < 2 else 1))

        def near_start(h):
            for o in range(1, NZ):
                own_copy(o, h, True).wait_recv()
            for oa in range(1, plan[h][0][0]):
                started(sent, functools.partial(near_copy, oa, h))

        def far_start(h):
            for oa in range(1, plan[h][0][0]):
                near_copy(oa, h, True).wait_recv()
            if ring:
                for to, zs in ((1, low), (3, high), (1, high), (3, low)):
                    started(last, functools.partial(far_copy, h, 0, zs, to))
            else:
                for ob in range(1, plan[h][1][0]):
                    started(last, functools.partial(far_copy, h, 0, every, ob))

        def far_middle(h):
            if ring:
                for origin, zs, to in ((3, low, 1), (1, high, 3)):
                    far_arrival(h, origin, zs, to).wait_recv()
                    started(last, functools.partial(far_copy, h, origin, zs, to))

        both_parts = range(PARTS)
        a_start()
        run(queue, beside[0])
        for h in both_parts:
            a_middle(h)
        run(queue, beside[1])
        for h in both_parts:
            a_close(h)
        run(queue, beside[2])
        for h in both_parts:
            b_close(h)
        run(queue, beside[3])
        for h in both_parts:
            z_close(h)
        run(queue, beside[4])
        for h in both_parts:
            near_start(h)
        run(queue, beside[5])
        for h in both_parts:
            far_start(h)
        run(queue, beside[6])
        for h in both_parts:
            far_middle(h)
        run(queue, len(queue))
        flush(sent)
        inverse_here(level + 1)
        total = jnp.zeros((2 * WIDTH, VECS), jnp.float32)

        def products(total, at):
            for ox, oy in at:
                total += product(level + 1, full, *plan[0][2](oy, ox))
            return total

        if ring:
            for h in both_parts:
                far_arrival(h, 3, high, 1).wait_recv()
                far_arrival(h, 1, low, 3).wait_recv()
            total = products(total, [(ox, oy) for ox in (0, 1, 3) for oy in (0, 1, 3)])
            for h in both_parts:
                far_arrival(h, 2, low, 2).wait_recv()
                far_arrival(h, 2, high, 2).wait_recv()
            total = products(total, [(ox, oy) for ox in range(4) for oy in range(4) if 2 in (ox, oy)])
        else:
            for h in both_parts:
                nb = plan[h][1][0]
                for ob in range(1, nb):
                    far_arrival(h, nb - ob, every, ob).wait_recv()
            total = products(total, [(ox, oy) for ox in range(nx) for oy in range(NY)])
        conclude(level + 1, total, out, last)

    def of_list(placed, which, first, at, rows):
        blocks = placed[pl.ds((first + at[0] * NY + at[1]) * NZ, NZ), rows]
        return jnp.dot(
            blocks.reshape(-1, 2 * WIDTH), solved[which], preferred_element_type=jnp.float32
        ).reshape(*blocks.shape[:2], VECS)

    full_two[0, y, z, c] = rhs_two[...].astype(jnp.bfloat16)
    blank(full_two)
    pl.semaphore_wait(barrier, len(greeted))
    root_blocks = placed_one.shape[0]

    def start_two():
        lower_copy(0).start()
        inverse_copy(0).start()
        loads[0].wait()
        invert(0)

    def start_one():
        lower_copy(1).start()
        inverse_copy(1).start()
        inverse_copy(2).start()
        loads[1].wait()
        invert(1)

    def wait_index(which):
        index_copy(which).wait()

    top()

    queue = [
        start_one, lambda: turn(1), *fetches(0, 0, root_blocks, 16), lambda: wait_index(1),
        *fetches(1, 0, root_blocks, 16),
    ]
    level_down(
        0, 2, lambda at, rows: of_list(placed_two, 0, ROOT_SLABS, at, rows), level_refs["one"],
        rhs_one, full_one, sol_one, queue, (3, 0, 2, 3, 3, 2, 2),
    )

    level_down(
        1, 4, lambda at, rows: of_list(placed_two, 0, 0, at, rows) + of_list(placed_one, 1, 0, at, rows),
        level_refs["root"], rhs_root, full_root, sol_root, [], (0,) * 7,
    )
    for which in range(2):
        lower_copy(which).wait_send()
    for level in range(3):
        inverse_copy(level).wait_send()


def substitute(rhs_root, rhs_one, rhs_two, inv_root, inv_one, inv_two, lower_two, lower_one, rows_two, rows_one, count_two, count_one):
    vmem = pl.BlockSpec(memory_space=pltpu.VMEM)
    smem = pl.BlockSpec(memory_space=pltpu.SMEM)
    hbm = pl.BlockSpec(memory_space=pl.ANY)
    bf16 = jnp.bfloat16
    length = lower_two.shape[1]
    blocks_one = inv_root.shape[1] // (NC * WIDTH)
    blocks_two = blocks_one + inv_one.shape[1] // (NC * WIDTH)

    def planes(*lead):
        return pltpu.VMEM((*lead, WIDTH, VECS), bf16)

    def level(nx):
        return [
            planes(3, NY, NZ), planes(3, NY, NZ), planes(NY, NZ), planes(3, NZ),
            pltpu.VMEM((NZ, WIDTH, VECS), jnp.float32), planes(NZ - 1),
        ]

    sems = pltpu.SemaphoreType.DMA
    out = jax.ShapeDtypeStruct((WIDTH, VECS), jnp.float32)
    return pl.pallas_call(
        main_kernel,
        out_shape=(out, out, out),
        in_specs=[vmem] * 3 + [hbm] * 7 + [smem] * 2,
        out_specs=(vmem,) * 3,
        scratch_shapes=[
            *[pltpu.VMEM((2 * WIDTH, inverse.shape[1]), bf16) for inverse in (inv_root, inv_one, inv_two)],
            pltpu.VMEM((2, NC, WIDTH, length), bf16),
            pltpu.VMEM((1, length), jnp.int32),
            pltpu.VMEM((1, length), jnp.int32),
            pltpu.VMEM((blocks_two, WIDTH), jnp.int32),
            pltpu.VMEM((blocks_one, WIDTH), jnp.int32),
            pltpu.SMEM((blocks_two, WIDTH), jnp.int32),
            pltpu.SMEM((blocks_one, WIDTH), jnp.int32),
            pltpu.VMEM((length + 8, 2 * WIDTH), jnp.float32),
            pltpu.VMEM((length + 8, 2 * WIDTH), jnp.float32),
            pltpu.VMEM((blocks_two, WIDTH, 2 * WIDTH), bf16),
            pltpu.VMEM((blocks_one, WIDTH, 2 * WIDTH), bf16),
            planes(1, NY, NZ, NC),
            planes(2, NY, NZ, NC),
            planes(NX, NY, NZ, NC),
            pltpu.VMEM((2, 2 * WIDTH, VECS), bf16),
            pltpu.VMEM((3, 2 * WIDTH, VECS), jnp.float32),
            pltpu.VMEM((3, 2 * WIDTH, VECS), jnp.float32),
            pltpu.VMEM((2 * WIDTH, VECS), jnp.float32),
            *level(2),
            *level(4),
            sems((9,)),
            sems((2, 2)),
            sems((2, 3)),
            sems((2, 3)),
            sems((2, 3, PARTS, NZ)),
            sems((2, 3, PARTS, 4)),
            sems((2, 3, PARTS, 4, 2)),
            sems((2, 2, PARTS, NZ)),
            sems((2, 2, PARTS, 4, 2)),
            sems((2, 2, PARTS, 4)),
        ],
        compiler_params=pltpu.CompilerParams(
            collective_id=0, has_side_effects=True, vmem_limit_bytes=60 * 2**20
        ),
    )(rhs_root, rhs_one, rhs_two, inv_root, inv_one, inv_two, lower_two, lower_one, rows_two, rows_one, count_two, count_one)


def hand_over_kernel(*refs):
    for given, out in zip(refs[:3], refs[3:]):
        out[...] = given[...]


def hand_over(arrays):
    vmem = pl.BlockSpec(memory_space=pltpu.VMEM)
    return pl.pallas_call(
        hand_over_kernel,
        out_shape=tuple(jax.ShapeDtypeStruct(array.shape, array.dtype) for array in arrays),
        in_specs=[vmem] * 3,
        out_specs=(vmem,) * 3,
    )(*arrays)


def shards(
    rhs_root,
    rhs_one,
    rhs_two,
    inv_root,
    inv_one,
    inv_two,
    lower_one,
    lower_two,
    rows_one,
    rows_two,
    count_one,
    count_two,
):
    solved = substitute(
        rhs_root.T, rhs_one.T, rhs_two.T, inv_root, inv_one, inv_two,
        lower_two, lower_one, rows_two, rows_one, count_two, count_one,
    )
    return tuple(array.T for array in hand_over(solved))


def solution(mesh):
    cut = P(None, ("leaf", "blk"))
    rows = P(("leaf", "blk"), None)
    return jax.shard_map(
        shards,
        mesh=mesh,
        in_specs=(cut, cut, cut, rows, rows, rows, rows, rows, P(), P(), P(), P()),
        out_specs=(cut, cut, cut),
        check_vma=False,
    )
```

```python
import functools

import jax
import jax.numpy as jnp
from jax import lax
from jax.experimental import pallas as pl
from jax.experimental.pallas import tpu as pltpu
from jax.sharding import PartitionSpec as P

VECS = 128
WIDTH = 64
MESH = pl.DeviceIdType.MESH
NX, NY, NZ, NC = 4, 4, 8, 2
ROOT_SLABS = NX * NY
PARTS = 4
FAR_FIRST = (4, 3, 5, 2, 6, 1, 7)
RING_ORDER = {2: (1,), 4: (2, 1, 3)}
TOP_ROWS = 48


def main_kernel(
    rhs_root, rhs_one, rhs_two, inv_root_hbm, inv_one_hbm, inv_two_hbm,
    lower_two_hbm, lower_one_hbm, rows_two_hbm, rows_one_hbm, count_two, count_one,
    sol_root, sol_one, sol_two,
    inv_root, inv_one, inv_two, lower, rows_two, rows_one,
    found_two, found_one, index_two, index_one, source_two, source_one, placed_two, placed_one,
    full_two, full_one, full_root, solved, mine, theirs, both,
    *rest,
):
    level_refs = {"one": rest[:6], "root": rest[6:12]}
    local_sems, lower_sems, inv_sems, part_sems, z_sems, a_sems, b_sems, rz_sems, ra_sems, rb_sems = rest[12:]
    leaf = lax.axis_index("leaf")
    blk = lax.axis_index("blk")
    x, y = leaf // NY, leaf % NY
    z, c = blk // NC, blk % NC
    half, pair = x // 2, x % 2
    other = 1 - c
    length = lower_two_hbm.shape[1]

    def z_peer(at):
        return (leaf, at * NC + c)

    sibling = (leaf, z * NC + other)

    inverses = ((inv_two_hbm, inv_two), (inv_one_hbm, inv_one), (inv_root_hbm, inv_root))
    my_rows, their_rows = pl.ds(c * WIDTH, WIDTH), pl.ds(other * WIDTH, WIDTH)
    loads = [
        pltpu.make_async_copy(rows_two_hbm.at[pl.ds(x, 1)], rows_two, local_sems.at[0]),
        pltpu.make_async_copy(rows_one_hbm.at[pl.ds(half, 1)], rows_one, local_sems.at[1]),
        pltpu.make_async_copy(lower_two_hbm, lower.at[0, c], local_sems.at[2]),
        pltpu.make_async_copy(lower_one_hbm, lower.at[1, c], local_sems.at[3]),
        *[
            pltpu.make_async_copy(hbm, inverse.at[my_rows], local_sems.at[4 + level])
            for level, (hbm, inverse) in enumerate(inverses)
        ],
    ]
    for load in loads:
        load.start()

    barrier = pltpu.get_barrier_semaphore()
    greeted = [z_peer((z + o) % NZ) for o in range(1, NZ)]
    greeted += [(x * NY + (y + o) % NY, blk) for o in range(1, NY)]
    greeted += [((x + o) % NX * NY + y, blk) for o in range(1, NX)]
    greeted += [sibling]
    for device in greeted:
        pl.semaphore_signal(barrier, inc=1, device_id=device, device_id_type=MESH)

    def remote(source, target, sems, index, device):
        return pltpu.make_async_remote_copy(
            src_ref=source,
            dst_ref=target,
            send_sem=sems.at[(0, *index)],
            recv_sem=sems.at[(1, *index)],
            device_id=device,
            device_id_type=MESH,
        )

    def axes_of(core, nx):
        mine_x = {1: 0, 2: pair, 4: x}[nx]

        def x_peer(o):
            to = half * 2 + (pair + o) % 2 if nx == 2 else (x + o) % NX
            return (to * NY + y, blk)

        def y_peer(o):
            return (x * NY + (y + o) % NY, blk)

        along_x, along_y = (nx, x_peer), (NY, y_peer)
        first, second = (along_y, along_x) if core == 0 else (along_x, along_y)

        def offsets(oa, ob):
            ox, oy = (ob, oa) if core == 0 else (oa, ob)
            return (mine_x + ox) % nx, (y + oy) % NY

        return first, second, offsets

    lists = (
        (rows_two, count_two, x, found_two, index_two, source_two, placed_two),
        (rows_one, count_one, half, found_one, index_one, source_one, placed_one),
    )

    def index_copy(which):
        return pltpu.make_async_copy(lists[which][3], lists[which][4], local_sems.at[7 + which])

    def invert(which):
        rows, counts, at, found, _, _, placed = lists[which]
        blocks, step = placed.shape[0], 1024
        count = counts[at]

        def body(i, total):
            row = rows[:, pl.ds(pl.multiple_of(i * step, step), step)]
            entry = lax.broadcasted_iota(jnp.int32, (1, step), 1) + i * step + 1
            block = jnp.where(entry <= count, row // 128, -1)
            within = row % 128 - c * WIDTH
            here = lax.broadcasted_iota(jnp.int32, (blocks, step), 0) == block
            mine = lax.broadcasted_iota(jnp.int32, (WIDTH, step), 0) == within
            upper = jnp.where(mine, (entry // 128).astype(jnp.float32), 0.0)
            lower_part = jnp.where(mine, (entry % 128).astype(jnp.float32), 0.0)
            digits = jnp.concatenate([upper, lower_part], axis=0).astype(jnp.bfloat16)
            return total + lax.dot_general(
                jnp.where(here, 1.0, 0.0).astype(jnp.bfloat16), digits, (((1,), (1,)), ((), ())),
                preferred_element_type=jnp.float32,
            )

        total = lax.fori_loop(0, length // step, body, jnp.zeros((blocks, 2 * WIDTH), jnp.float32))
        entry = (total[:, :WIDTH] * 128.0 + total[:, WIDTH:]).astype(jnp.int32)
        found[...] = jnp.clip(jnp.where(entry > 0, entry - 1, length), 0, length)
        index_copy(which).start()

    def lower_copy(which):
        hbm = (lower_two_hbm, lower_one_hbm)[which]
        return remote(hbm, lower.at[which, c], lower_sems, (which,), sibling)

    def lower_arrival(which):
        return remote(lower.at[which, other], lower.at[which, other], lower_sems, (which,), sibling)

    def inverse_copy(level):
        hbm, inverse = inverses[level]
        return remote(hbm, inverse.at[my_rows], inv_sems, (level,), sibling)

    def inverse_here(level):
        inverse = inverses[level][1]
        loads[4 + level].wait()
        remote(inverse.at[their_rows], inverse.at[their_rows], inv_sems, (level,), sibling).wait_recv()

    def turn(which):
        source, step = lists[which][5], 512
        loads[2 + which].wait()
        lower_arrival(which).wait_recv()

        def body(i, carry):
            cols = pl.ds(pl.multiple_of(i * step, step), step)
            both = jnp.concatenate([lower[which, 0, :, cols], lower[which, 1, :, cols]], axis=0)
            source[cols, :] = both.astype(jnp.float32).T
            return carry

        lax.fori_loop(0, length // step, body, 0)
        source[length:, :] = jnp.zeros((source.shape[0] - length, 2 * WIDTH), jnp.float32)

    def fetch(which, start, stop):
        _, _, _, _, index, source, placed = lists[which]

        def body(block, carry):
            picked = [source[pl.ds(index[block, k], 1), :] for k in range(WIDTH)]
            placed[block] = jnp.concatenate(picked, axis=0).astype(jnp.bfloat16)
            return carry

        lax.fori_loop(start, stop, body, 0)

    def fetches(which, start, stop, step):
        return [functools.partial(fetch, which, at, at + step) for at in range(start, stop, step)]

    def run(queue, count):
        for _ in range(min(count, len(queue))):
            queue.pop(0)()

    def blank(full):
        def body(slab, carry):
            full[slab // NY, slab % NY, :, other] = jnp.zeros((NZ, WIDTH, VECS), jnp.bfloat16)
            return carry

        lax.fori_loop(0, full.shape[0] * NY, body, 0)

    def part_of(h):
        return slice(h * WIDTH // PARTS, (h + 1) * WIDTH // PARTS)

    def started(sent, make):
        make().start()
        sent.append(make)

    def flush(sent):
        while sent:
            sent.pop(0)().wait_send()

    def product(level, full, at_x, at_y):
        wide = NZ * NC * WIDTH
        slab = at_x * NY + at_y
        return jnp.dot(
            inverses[level][1][:, pl.ds(pl.multiple_of(slab * wide, wide), wide)],
            full[at_x, at_y].reshape(wide, VECS),
            preferred_element_type=jnp.float32,
        )

    def conclude(level, total, out, sent):
        mine[level] = total
        partial = remote(mine.at[level], theirs.at[level], part_sems, (level,), sibling)
        partial.start()
        flush(sent)
        partial.wait()
        total = mine[level] + theirs[level]
        both[...] = total
        out[...] = both[my_rows]
        if level < 2:
            solved[level] = total.astype(jnp.bfloat16)

    def top():
        sent = []
        rows = (slice(0, TOP_ROWS), slice(TOP_ROWS, WIDTH))

        def z_copy(h, o, arrival=False):
            at = (z + NZ - o) % NZ if arrival else z
            block = full_two.at[0, slice(None) if h else y, at, c, rows[h]]
            return remote(block, block, z_sems, (0, h, o), z_peer((z + o) % NZ))

        def y_copy(h, o, arrival=False):
            at = (y + NY - o) % NY if arrival else y
            block = full_two.at[0, at, z if h else slice(None), c, rows[h]]
            return remote(block, block, a_sems, (0, h, o), (x * NY + (y + o) % NY, blk))

        along_z = lambda h: [functools.partial(z_copy, h, o) for o in FAR_FIRST]
        along_y = lambda h: [functools.partial(y_copy, h, o) for o in range(1, NY)]
        for make in along_y(1) + along_z(0):
            started(sent, make)
        start_two()
        for first, second in ((along_y(1), along_z(1)), (along_z(0), along_y(0))):
            for make in first:
                make(True).wait_recv()
            for make in second:
                started(sent, make)
        blank(full_one)
        blank(full_root)
        turn(0)
        wait_index(0)
        fetch(0, root_blocks, placed_two.shape[0])
        inverse_here(0)
        for make in along_y(0) + along_z(1):
            make(True).wait_recv()
        total = jnp.zeros((2 * WIDTH, VECS), jnp.float32)
        for at_y in range(NY):
            total += product(0, full_two, 0, at_y)
        conclude(0, total, sol_two, sent)

    def level_down(level, nx, terms, refs, rhs, full, out, queue, beside):
        sums, ra, totals, rb, whole, landed = refs
        sent, last = [], []
        plan = [axes_of(h % 2, nx) for h in range(PARTS)]
        ring = nx == 4
        low, high, every = slice(0, NZ // 2), slice(NZ // 2, NZ), slice(None)

        def a_copy(h, oa, zs, target, to):
            (_, a_peer), (nb, _), _ = plan[h]
            at = (slice(0, nb), zs, part_of(h))
            return remote(
                sums.at[(oa - 1, *at)], ra.at[(target - 1, *at)], ra_sems,
                (level, h, oa, {low: 0, high: 1, every: 0}[zs]), a_peer(to),
            )

        def b_copy(ob, h):
            return remote(
                totals.at[ob, :, part_of(h)], rb.at[ob - 1, :, part_of(h)], rb_sems, (level, h, ob), plan[h][1][1](ob)
            )

        def z_copy(o, h):
            return remote(
                totals.at[0, (z + o) % NZ, part_of(h)], landed.at[o - 1, part_of(h)], rz_sems, (level, h, o),
                z_peer((z + o) % NZ),
            )

        def make(h, oa):
            for ob in range(plan[h][1][0]):
                sums[oa - 1, ob, :, part_of(h)] = terms(plan[h][2](oa, ob), part_of(h)).astype(jnp.bfloat16)

        def a_start():
            if not ring:
                for h in range(PARTS):
                    for oa in RING_ORDER[plan[h][0][0]]:
                        make(h, oa)
                        started(sent, functools.partial(a_copy, h, oa, every, oa, oa))
                return
            for h in range(PARTS):
                make(h, 2)
                started(sent, functools.partial(a_copy, h, 2, low, 2, 1))
                started(sent, functools.partial(a_copy, h, 2, high, 2, 3))
            for h in range(PARTS):
                for oa, zs in ((1, high), (3, low)):
                    make(h, oa)
                    started(sent, functools.partial(a_copy, h, oa, zs, oa, oa))

        def a_middle(h):
            if ring:
                for oa, zs, to in ((1, low, 1), (3, high, 3)):
                    a_copy(h, 2, zs, 2, to).wait_recv()
                    at = (slice(0, NY), zs, part_of(h))
                    joined = sums[(oa - 1, *at)].astype(jnp.float32) + ra[(1, *at)].astype(jnp.float32)
                    sums[(oa - 1, *at)] = joined.astype(jnp.bfloat16)
                    started(sent, functools.partial(a_copy, h, oa, zs, oa, oa))

        def a_close(h):
            (na, _), (nb, _), offsets = plan[h]
            rows = part_of(h)
            for oa in (1, 3) if ring else range(1, na):
                for zs in (low, high) if ring else (every,):
                    a_copy(h, oa, zs, oa, oa).wait_recv()
            for ob in [*RING_ORDER[nb], 0]:
                value = terms(offsets(0, ob), rows)
                for oa in (1, 3) if ring else range(1, na):
                    value += ra[oa - 1, ob, :, rows].astype(jnp.float32)
                if ob:
                    totals[ob, :, rows] = value.astype(jnp.bfloat16)
                    started(sent, functools.partial(b_copy, ob, h))
                else:
                    whole[:, rows] = value

        def b_close(h):
            rows = part_of(h)
            value = whole[:, rows]
            for ob in range(1, plan[h][1][0]):
                b_copy(ob, h).wait_recv()
                value += rb[ob - 1, :, rows].astype(jnp.float32)
            whole[:, rows] = value
            totals[0, :, rows] = value.astype(jnp.bfloat16)
            for o in FAR_FIRST:
                started(sent, functools.partial(z_copy, o, h))

        def z_close(h):
            rows = part_of(h)
            value = whole[z, rows]
            for o in range(1, NZ):
                z_copy(o, h).wait_recv()
                value += landed[o - 1, rows].astype(jnp.float32)
            at_x, at_y = plan[h][2](0, 0)
            full[at_x, at_y, z, c, rows] = (rhs[rows] - value).astype(jnp.bfloat16)
            for o in FAR_FIRST:
                started(sent, functools.partial(own_copy, o, h))

        def own_copy(o, h, arrival=False):
            at = (z + NZ - o) % NZ if arrival else z
            block = full.at[(*plan[h][2](0, 0), at, c, part_of(h))]
            return remote(block, block, z_sems, (level + 1, h, o), z_peer((z + o) % NZ))

        def near_copy(oa, h, arrival=False):
            (na, a_peer), _, offsets = plan[h]
            block = full.at[(*offsets(na - oa if arrival else 0, 0), every, c, part_of(h))]
            return remote(block, block, a_sems, (level + 1, h, oa), a_peer(oa))

        def far_copy(h, origin, zs, to):
            (_, b_peer), offsets = plan[h][1:]
            at_x, at_y = offsets(0, origin)
            line = (at_x, every) if h % 2 == 0 else (every, at_y)
            block = full.at[(*line, zs, c, part_of(h))]
            kind = to if origin == 0 else 2
            return remote(
                block, block, b_sems, (level + 1, h, kind, {low: 0, high: 1, every: 0}[zs]), b_peer(to)
            )

        def far_arrival(h, ob, zs, by):
            (nb, b_peer), offsets = plan[h][1:]
            at_x, at_y = offsets(0, ob)
            line = (at_x, every) if h % 2 == 0 else (every, at_y)
            block = full.at[(*line, zs, c, part_of(h))]
            return remote(block, block, b_sems, (level + 1, h, by, {low: 0, high: 1, every: 0}[zs]), b_peer(0 if nb < 2 else 1))

        def near_start(h):
            for o in range(1, NZ):
                own_copy(o, h, True).wait_recv()
            for oa in RING_ORDER[plan[h][0][0]]:
                started(sent, functools.partial(near_copy, oa, h))

        def far_start(h):
            for oa in range(1, plan[h][0][0]):
                near_copy(oa, h, True).wait_recv()
            if ring:
                for to, zs in ((1, low), (3, high), (1, high), (3, low)):
                    started(last, functools.partial(far_copy, h, 0, zs, to))
            else:
                for ob in RING_ORDER[plan[h][1][0]]:
                    started(last, functools.partial(far_copy, h, 0, every, ob))

        def far_middle(h):
            if ring:
                for origin, zs, to in ((3, low, 1), (1, high, 3)):
                    far_arrival(h, origin, zs, to).wait_recv()
                    started(last, functools.partial(far_copy, h, origin, zs, to))

        both_parts = range(PARTS)
        a_start()
        run(queue, beside[0])
        for h in both_parts:
            a_middle(h)
        run(queue, beside[1])
        for h in both_parts:
            a_close(h)
        run(queue, beside[2])
        for h in both_parts:
            b_close(h)
        run(queue, beside[3])
        for h in both_parts:
            z_close(h)
        run(queue, beside[4])
        for h in both_parts:
            near_start(h)
        run(queue, beside[5])
        for h in both_parts:
            far_start(h)
        run(queue, beside[6])
        for h in both_parts:
            far_middle(h)
        run(queue, len(queue))
        flush(sent)
        inverse_here(level + 1)
        total = jnp.zeros((2 * WIDTH, VECS), jnp.float32)

        def products(total, at):
            for ox, oy in at:
                total += product(level + 1, full, *plan[0][2](oy, ox))
            return total

        if ring:
            for h in both_parts:
                far_arrival(h, 3, high, 1).wait_recv()
                far_arrival(h, 1, low, 3).wait_recv()
            total = products(total, [(ox, oy) for ox in (0, 1, 3) for oy in (0, 1, 3)])
            for h in both_parts:
                far_arrival(h, 2, low, 2).wait_recv()
                far_arrival(h, 2, high, 2).wait_recv()
            total = products(total, [(ox, oy) for ox in range(4) for oy in range(4) if 2 in (ox, oy)])
        else:
            for h in both_parts:
                nb = plan[h][1][0]
                for ob in range(1, nb):
                    far_arrival(h, nb - ob, every, ob).wait_recv()
            total = products(total, [(ox, oy) for ox in range(nx) for oy in range(NY)])
        conclude(level + 1, total, out, last)

    def of_list(placed, which, first, at, rows):
        blocks = placed[pl.ds((first + at[0] * NY + at[1]) * NZ, NZ), rows]
        return jnp.dot(
            blocks.reshape(-1, 2 * WIDTH), solved[which], preferred_element_type=jnp.float32
        ).reshape(*blocks.shape[:2], VECS)

    full_two[0, y, z, c] = rhs_two[...].astype(jnp.bfloat16)
    blank(full_two)
    pl.semaphore_wait(barrier, len(greeted))
    root_blocks = placed_one.shape[0]

    def start_two():
        lower_copy(0).start()
        inverse_copy(0).start()
        loads[0].wait()
        invert(0)

    def start_one():
        lower_copy(1).start()
        inverse_copy(1).start()
        inverse_copy(2).start()
        loads[1].wait()
        invert(1)

    def wait_index(which):
        index_copy(which).wait()

    top()

    queue = [
        start_one, lambda: turn(1), *fetches(0, 0, root_blocks, 16), lambda: wait_index(1),
        *fetches(1, 0, root_blocks, 16),
    ]
    level_down(
        0, 2, lambda at, rows: of_list(placed_two, 0, ROOT_SLABS, at, rows), level_refs["one"],
        rhs_one, full_one, sol_one, queue, (3, 0, 2, 3, 3, 2, 2),
    )

    level_down(
        1, 4, lambda at, rows: of_list(placed_two, 0, 0, at, rows) + of_list(placed_one, 1, 0, at, rows),
        level_refs["root"], rhs_root, full_root, sol_root, [], (0,) * 7,
    )
    for which in range(2):
        lower_copy(which).wait_send()
    for level in range(3):
        inverse_copy(level).wait_send()


def substitute(rhs_root, rhs_one, rhs_two, inv_root, inv_one, inv_two, lower_two, lower_one, rows_two, rows_one, count_two, count_one):
    vmem = pl.BlockSpec(memory_space=pltpu.VMEM)
    smem = pl.BlockSpec(memory_space=pltpu.SMEM)
    hbm = pl.BlockSpec(memory_space=pl.ANY)
    bf16 = jnp.bfloat16
    length = lower_two.shape[1]
    blocks_one = inv_root.shape[1] // (NC * WIDTH)
    blocks_two = blocks_one + inv_one.shape[1] // (NC * WIDTH)

    def planes(*lead):
        return pltpu.VMEM((*lead, WIDTH, VECS), bf16)

    def level(nx):
        return [
            planes(3, NY, NZ), planes(3, NY, NZ), planes(NY, NZ), planes(3, NZ),
            pltpu.VMEM((NZ, WIDTH, VECS), jnp.float32), planes(NZ - 1),
        ]

    sems = pltpu.SemaphoreType.DMA
    out = jax.ShapeDtypeStruct((WIDTH, VECS), jnp.float32)
    return pl.pallas_call(
        main_kernel,
        out_shape=(out, out, out),
        in_specs=[vmem] * 3 + [hbm] * 7 + [smem] * 2,
        out_specs=(vmem,) * 3,
        scratch_shapes=[
            *[pltpu.VMEM((2 * WIDTH, inverse.shape[1]), bf16) for inverse in (inv_root, inv_one, inv_two)],
            pltpu.VMEM((2, NC, WIDTH, length), bf16),
            pltpu.VMEM((1, length), jnp.int32),
            pltpu.VMEM((1, length), jnp.int32),
            pltpu.VMEM((blocks_two, WIDTH), jnp.int32),
            pltpu.VMEM((blocks_one, WIDTH), jnp.int32),
            pltpu.SMEM((blocks_two, WIDTH), jnp.int32),
            pltpu.SMEM((blocks_one, WIDTH), jnp.int32),
            pltpu.VMEM((length + 8, 2 * WIDTH), jnp.float32),
            pltpu.VMEM((length + 8, 2 * WIDTH), jnp.float32),
            pltpu.VMEM((blocks_two, WIDTH, 2 * WIDTH), bf16),
            pltpu.VMEM((blocks_one, WIDTH, 2 * WIDTH), bf16),
            planes(1, NY, NZ, NC),
            planes(2, NY, NZ, NC),
            planes(NX, NY, NZ, NC),
            pltpu.VMEM((2, 2 * WIDTH, VECS), bf16),
            pltpu.VMEM((3, 2 * WIDTH, VECS), jnp.float32),
            pltpu.VMEM((3, 2 * WIDTH, VECS), jnp.float32),
            pltpu.VMEM((2 * WIDTH, VECS), jnp.float32),
            *level(2),
            *level(4),
            sems((9,)),
            sems((2, 2)),
            sems((2, 3)),
            sems((2, 3)),
            sems((2, 3, PARTS, NZ)),
            sems((2, 3, PARTS, 4)),
            sems((2, 3, PARTS, 4, 2)),
            sems((2, 2, PARTS, NZ)),
            sems((2, 2, PARTS, 4, 2)),
            sems((2, 2, PARTS, 4)),
        ],
        compiler_params=pltpu.CompilerParams(
            collective_id=0, has_side_effects=True, vmem_limit_bytes=60 * 2**20
        ),
    )(rhs_root, rhs_one, rhs_two, inv_root, inv_one, inv_two, lower_two, lower_one, rows_two, rows_one, count_two, count_one)


def hand_over_kernel(*refs):
    for given, out in zip(refs[:3], refs[3:]):
        out[...] = given[...]


def hand_over(arrays):
    vmem = pl.BlockSpec(memory_space=pltpu.VMEM)
    return pl.pallas_call(
        hand_over_kernel,
        out_shape=tuple(jax.ShapeDtypeStruct(array.shape, array.dtype) for array in arrays),
        in_specs=[vmem] * 3,
        out_specs=(vmem,) * 3,
    )(*arrays)


def shards(
    rhs_root,
    rhs_one,
    rhs_two,
    inv_root,
    inv_one,
    inv_two,
    lower_one,
    lower_two,
    rows_one,
    rows_two,
    count_one,
    count_two,
):
    solved = substitute(
        rhs_root.T, rhs_one.T, rhs_two.T, inv_root, inv_one, inv_two,
        lower_two, lower_one, rows_two, rows_one, count_two, count_one,
    )
    return tuple(array.T for array in hand_over(solved))


def solution(mesh):
    cut = P(None, ("leaf", "blk"))
    rows = P(("leaf", "blk"), None)
    return jax.shard_map(
        shards,
        mesh=mesh,
        in_specs=(cut, cut, cut, rows, rows, rows, rows, rows, P(), P(), P(), P()),
        out_specs=(cut, cut, cut),
        check_vma=False,
    )
```
